128 devices in a mesh: cell: 8 (over z, core), tile: 16 (over x, y).
Axes of the slice: x: 4, y: 4, z: 4, core: 2. Of those that a mesh axis runs over, the one named last changes fastest.
Arguments:
- gaussians: float32 [59, 1048576], P(None, ('cell', 'tile'))
- send_index: int32 [128, 128, 128], P(('cell', 'tile')), may hold values from 0 to 8191, as said below
- tile_slots: int32 [4096, 4, 256], P(('cell', 'tile')), may hold values from 0 to 16383, as said below
- block_count: int32 [4096], P(('cell', 'tile')), may hold values from 1 to 4, as said below
- cotangent: float32 [3, 4096, 256], P(None, ('cell', 'tile')), may hold values from -6 to 6
Outputs:
- image: float32 [3, 4096, 256], P(None, ('cell', 'tile'))
- sh_grad: float32 [48, 1048576], P(None, ('cell', 'tile'))
The draws below stay inside these ranges and needn't reach their ends.
Inputs may be any that keep to these rules, and one draw needn't show every extreme that they name: `block_count`: every tile has 1 to 4 live blocks, and some tile has exactly 4. `send_index`: a local Gaussian index of the owner. `tile_slots`: a slot of the tile's renderer.
All inputs are finite; a program needn't handle non-finite values.
Results may differ from the reference program's by a relative error of at most 0.0003.
Values sent between devices are 32-bit elements; how exact they have to be, the bound alone decides.
No kernel may reach another device: no remote copies, remote signals or barrier semaphores. Data moves between devices by JAX's collectives and lax.ppermute only.
A program may use at most 128 MiB of HBM per device.

```python
import jax
import jax.numpy as jnp
from jax import lax

SHC = 48
TILE_PIX = 256
GBLOCK = 256
BLOCKS = 4
G_DEV = 8192
C = 128
TILE_DEV = 32
DEVICES_ALL = 128
GAUSS = 1048576
TILES = 4096
SLOTS = 16384


def draw_lists(key):
    send_index = jax.random.randint(jax.random.fold_in(key, 101), (DEVICES_ALL, DEVICES_ALL, C), 0, G_DEV).astype(jnp.int32)
    tile_slots = jax.random.randint(jax.random.fold_in(key, 102), (TILES, BLOCKS, GBLOCK), 0, SLOTS).astype(jnp.int32)
    level = jax.random.randint(jax.random.fold_in(key, 103), (DEVICES_ALL, 1), 1, BLOCKS + 1)
    spread = jax.random.randint(jax.random.fold_in(key, 104), (DEVICES_ALL, TILE_DEV), 0, BLOCKS)
    counts = (1 + spread % level).reshape(TILES).astype(jnp.int32)
    chosen = jax.random.randint(jax.random.fold_in(key, 105), (), 0, TILES)
    counts = counts.at[chosen].set(BLOCKS).astype(jnp.int32)
    return (send_index, tile_slots, counts)


def draw_gaussians(key, part):
    send_index, tile_slots, counts = draw_lists(key)
    key = jax.random.fold_in(key, 1)
    subkeys = jax.random.split(key, 10)
    tiles_here = jnp.arange(TILES, dtype=jnp.int32)[:, None, None]
    owner = tile_slots // C
    renderer = tiles_here // TILE_DEV
    listed = owner * G_DEV + send_index[owner, renderer, tile_slots % C]
    live = (jnp.arange(BLOCKS, dtype=jnp.int32)[None, :, None] < counts[:, None, None]).astype(jnp.int32)
    priority = jax.random.randint(subkeys[7], tile_slots.shape, 0, 32768).astype(jnp.int32)
    score = (live * 32768 + priority) * TILES + tiles_here
    best = jnp.full((GAUSS,), -1, jnp.int32).at[listed.reshape(-1)].max(score.reshape(-1))
    fallback = jax.random.randint(subkeys[8], (GAUSS,), 0, TILES).astype(jnp.int32)
    home = jnp.where(best >= 0, best % TILES, fallback)
    local_tile = home % 256
    centre_u = (16 * (local_tile % 16)).astype(jnp.float32) + jax.random.uniform(subkeys[0], (GAUSS,), jnp.float32, -2.0, 18.0)
    centre_v = (16 * (local_tile // 16)).astype(jnp.float32) + jax.random.uniform(subkeys[1], (GAUSS,), jnp.float32, -2.0, 18.0)
    depth = jax.random.uniform(subkeys[2], (1, GAUSS), jnp.float32, 2.0, 8.0)
    lateral = jnp.stack([(centre_u - 128.0) / 256.0, (centre_v - 128.0) / 256.0]) * depth
    log_scale = jax.random.uniform(subkeys[3], (3, GAUSS), jnp.float32, -6.5, -5.0)
    quat_real = jax.random.uniform(subkeys[4], (1, GAUSS), jnp.float32, 0.5, 1.0)
    quat_vector = jax.random.uniform(subkeys[5], (3, GAUSS), jnp.float32, -1.0, 1.0)
    logit = jax.random.uniform(subkeys[6], (1, GAUSS), jnp.float32, -1.5, 1.5)
    coefs = 0.3 * jax.random.normal(subkeys[9], (48, GAUSS), jnp.float32)
    return jnp.concatenate([lateral, depth, log_scale, quat_real, quat_vector, logit, coefs], axis=0)


def draw_send_index(key, part):
    send_index, tile_slots, counts = draw_lists(key)
    return send_index


def draw_tile_slots(key, part):
    send_index, tile_slots, counts = draw_lists(key)
    return tile_slots


def draw_block_count(key, part):
    send_index, tile_slots, counts = draw_lists(key)
    return counts


def levels(stream_key, dims, cuts, smallest, high):
    factor_of, own = 1.0, jax.random.fold_in(stream_key, 6)
    for position, shards_of in cuts:
        heights = jnp.exp(jax.random.uniform(jax.random.fold_in(own, position), (shards_of,), jnp.float32, smallest / len(cuts), high / len(cuts)))
        factor_of = factor_of * jnp.repeat(heights, dims[position] // shards_of).reshape([-1 if axis == position else 1 for axis in range(len(dims))])
    return factor_of


def centred(stream_key, shape, width, most, cuts=(), kind=jnp.bfloat16):
    result = width * jax.random.normal(stream_key, shape, jnp.float32)
    if cuts:
        result = result * levels(stream_key, shape, cuts, -0.22, 0.18)
    return jnp.clip(result, -most, most).astype(kind)


def setup_inputs(seed: int = 0) -> dict:
    streams_of = jax.random.split(jax.random.key(seed), 6)
    gaussians = draw_gaussians(jax.random.fold_in(streams_of[5], 71), 0)
    send_index = draw_send_index(jax.random.fold_in(streams_of[5], 71), 0)
    tile_slots = draw_tile_slots(jax.random.fold_in(streams_of[5], 71), 0)
    block_count = draw_block_count(jax.random.fold_in(streams_of[5], 71), 0)
    cotangent = centred(streams_of[4], (3, TILES, TILE_PIX), 1.0, 6.0, ((1, 128),), jnp.float32)
    return {"gaussians": gaussians, "send_index": send_index, "tile_slots": tile_slots, "block_count": block_count, "cotangent": cotangent}


FOCAL_LENGTH = 256.0
CENTRE_SHIFT = 128.0
BLUR_TERM = 0.3
HARM_ZERO = 0.28209479177387814
HARM_ONE = 0.4886025119029199
HARM_TWO = (1.0925484305920792, -1.0925484305920792, 0.31539156525252005, -1.0925484305920792, 0.5462742152960396)
HARM_THREE = (-0.5900435899266435, 2.890611442640554, -0.4570457994644658, 0.3731763325901154, -0.4570457994644658, 1.445305721320277, -0.5900435899266435)

def sh_basis(mean_x, mean_y, mean_z):
    inverse_norm = 1.0 / jnp.sqrt(mean_x * mean_x + mean_y * mean_y + mean_z * mean_z)
    unit_x = mean_x * inverse_norm
    unit_y = mean_y * inverse_norm
    unit_z = mean_z * inverse_norm
    square_x = unit_x * unit_x
    square_y = unit_y * unit_y
    square_z = unit_z * unit_z
    return jnp.stack([HARM_ZERO * jnp.ones_like(unit_x), -HARM_ONE * unit_y, HARM_ONE * unit_z, -HARM_ONE * unit_x, HARM_TWO[0] * unit_x * unit_y, HARM_TWO[1] * unit_y * unit_z, HARM_TWO[2] * (2.0 * square_z - square_x - square_y), HARM_TWO[3] * unit_x * unit_z, HARM_TWO[4] * (square_x - square_y), HARM_THREE[0] * unit_y * (3.0 * square_x - square_y), HARM_THREE[1] * unit_x * unit_y * unit_z, HARM_THREE[2] * unit_y * (4.0 * square_z - square_x - square_y), HARM_THREE[3] * unit_z * (2.0 * square_z - 3.0 * square_x - 3.0 * square_y), HARM_THREE[4] * unit_x * (4.0 * square_z - square_x - square_y), HARM_THREE[5] * unit_z * (square_x - square_y), HARM_THREE[6] * unit_x * (square_x - 3.0 * square_y)])

def project(params):
    mean_x, mean_y, mean_z = (params[0], params[1], params[2])
    scales = jnp.exp(params[3:6])
    quat_norm = jnp.sqrt(lax.optimization_barrier(jnp.sum(params[6:10] * params[6:10], axis=0)))
    quat_w = params[6] / quat_norm
    quat_x = params[7] / quat_norm
    quat_y = params[8] / quat_norm
    quat_z = params[9] / quat_norm
    rotation = [[1.0 - 2.0 * (quat_y * quat_y + quat_z * quat_z), 2.0 * (quat_x * quat_y - quat_w * quat_z), 2.0 * (quat_x * quat_z + quat_w * quat_y)], [2.0 * (quat_x * quat_y + quat_w * quat_z), 1.0 - 2.0 * (quat_x * quat_x + quat_z * quat_z), 2.0 * (quat_y * quat_z - quat_w * quat_x)], [2.0 * (quat_x * quat_z - quat_w * quat_y), 2.0 * (quat_y * quat_z + quat_w * quat_x), 1.0 - 2.0 * (quat_x * quat_x + quat_y * quat_y)]]
    scaled = [[rotation[row][col] * scales[col] for col in range(3)] for row in range(3)]
    sigma = [[sum((scaled[row][inner] * scaled[col][inner] for inner in range(3))) for col in range(3)] for row in range(3)]
    inverse_depth = 1.0 / mean_z
    jac_diag = FOCAL_LENGTH * inverse_depth
    jac_first = -FOCAL_LENGTH * mean_x * inverse_depth * inverse_depth
    jac_second = -FOCAL_LENGTH * mean_y * inverse_depth * inverse_depth
    upper_row = [jac_diag * sigma[0][col] + jac_first * sigma[2][col] for col in range(3)]
    lower_row = [jac_diag * sigma[1][col] + jac_second * sigma[2][col] for col in range(3)]
    entry_a = upper_row[0] * jac_diag + upper_row[2] * jac_first + BLUR_TERM
    entry_b = upper_row[1] * jac_diag + upper_row[2] * jac_second
    entry_c = lower_row[1] * jac_diag + lower_row[2] * jac_second + BLUR_TERM
    determinant = entry_a * entry_c - entry_b * entry_b
    centre_u = FOCAL_LENGTH * mean_x * inverse_depth + CENTRE_SHIFT
    centre_v = FOCAL_LENGTH * mean_y * inverse_depth + CENTRE_SHIFT
    opacity = 1.0 / (1.0 + jnp.exp(-params[10]))
    basis = sh_basis(mean_x, mean_y, mean_z)
    coefs = params[11:59].reshape(3, 16, -1)
    colour = 0.5 + lax.optimization_barrier(jnp.sum(coefs * basis[None], axis=1))
    attributes = jnp.stack([centre_u, centre_v, entry_c / determinant, -entry_b / determinant, entry_a / determinant, opacity, colour[0], colour[1], colour[2]])
    return (attributes, basis)

def render_block(attributes, slot_ids, tile_ids, live, cot_part, log_trans):
    picked = attributes[:, slot_ids]
    local_tile = tile_ids % 256
    pixel = jnp.arange(256, dtype=jnp.int32)
    pos_x = (16 * (local_tile % 16))[:, None].astype(jnp.float32) + (pixel % 16).astype(jnp.float32)[None, :] + 0.5
    pos_y = (16 * (local_tile // 16))[:, None].astype(jnp.float32) + (pixel // 16).astype(jnp.float32)[None, :] + 0.5
    delta_x = pos_x[:, :, None] - picked[0][:, None, :]
    delta_y = pos_y[:, :, None] - picked[1][:, None, :]
    power = -0.5 * (picked[2][:, None, :] * delta_x * delta_x + 2.0 * picked[3][:, None, :] * delta_x * delta_y + picked[4][:, None, :] * delta_y * delta_y)
    alpha = picked[5][:, None, :] * jnp.exp(power) * live[:, None, None]
    log_keep = jnp.log1p(-alpha)
    earlier = jnp.cumsum(log_keep, axis=2) - log_keep
    weight = alpha * jnp.exp(log_trans[:, :, None] + earlier)
    colour_part = jnp.einsum('npg,cng->cnp', weight, picked[6:9], precision=lax.Precision.HIGHEST)
    colour_grad = jnp.einsum('npg,cnp->cng', weight, cot_part, precision=lax.Precision.HIGHEST)
    return (log_trans + lax.optimization_barrier(jnp.sum(log_keep, axis=2)), colour_part, colour_grad)

def reference(gaussians, send_index, tile_slots, block_count, cotangent):
    attr_all, basis_all = project(gaussians)
    owner = jnp.arange(SLOTS, dtype=jnp.int32) // C
    column = jnp.arange(SLOTS, dtype=jnp.int32) % C

    def one_renderer(color_grad, rank):
        picks = send_index[owner, rank, column]
        global_ids = (owner * G_DEV + picks).astype(jnp.int32)
        attributes = attr_all[:, global_ids]
        start = (rank * TILE_DEV).astype(jnp.int32)
        slot_block = lax.dynamic_slice_in_dim(tile_slots, start, TILE_DEV, 0)
        counts = lax.dynamic_slice_in_dim(block_count, start, TILE_DEV, 0)
        cot_part = lax.dynamic_slice_in_dim(cotangent, start, TILE_DEV, 1)
        tile_ids = start + jnp.arange(TILE_DEV, dtype=jnp.int32)
        log_trans = jnp.zeros((TILE_DEV, TILE_PIX), jnp.float32)
        picture = jnp.zeros((3, TILE_DEV, TILE_PIX), jnp.float32)
        slot_grad = jnp.zeros((3, SLOTS), jnp.float32)
        for block in range(BLOCKS):
            live = (counts > block).astype(jnp.float32)
            log_trans, colour_part, colour_grad = render_block(attributes, slot_block[:, block], tile_ids, live, cot_part, log_trans)
            picture = picture + colour_part
            slot_grad = slot_grad.at[:, slot_block[:, block].reshape(-1)].add(colour_grad.reshape(3, -1))
        color_grad = color_grad.at[:, global_ids].add(slot_grad)
        return (color_grad, picture)
    color_grad, pictures = lax.scan(one_renderer, jnp.zeros((3, GAUSS), jnp.float32), jnp.arange(DEVICES_ALL, dtype=jnp.int32))
    image = jnp.transpose(pictures, (1, 0, 2, 3)).reshape(3, TILES, TILE_PIX)
    sh_grad = (basis_all[None] * color_grad[:, None]).reshape(SHC, GAUSS)
    return (image, sh_grad)
```

```python
import jax
import jax.numpy as jnp
from jax import lax
from jax.experimental import pallas as pl
from jax.experimental.pallas import tpu as pltpu
from jax.sharding import PartitionSpec as P

AXES = ("cell", "tile")
PEERS = 128
WIDTH = 128
OWNED = 8192
SLOTS = 16384
TILE_DEV = 32
BLOCKS = 4
PARAMS = 59
ATTRS = 9
UNIT = 256
Q_OWN = OWNED // UNIT
Q_SLOT = SLOTS // UNIT
LANES = 128
PAD_PARAMS = 64
F32 = jnp.float32
BF16 = jnp.bfloat16
VMEM_BYTES = 48 * 2**20

FOCAL_LENGTH = 256.0
CENTRE_SHIFT = 128.0
BLUR_TERM = 0.3
LOG2E = 1.4426950408889634
HARM_ZERO = 0.28209479177387814
HARM_ONE = 0.4886025119029199
HARM_TWO = (
    1.0925484305920792,
    -1.0925484305920792,
    0.31539156525252005,
    -1.0925484305920792,
    0.5462742152960396,
)
HARM_THREE = (
    -0.5900435899266435,
    2.890611442640554,
    -0.4570457994644658,
    0.3731763325901154,
    -0.4570457994644658,
    1.445305721320277,
    -0.5900435899266435,
)


def sh_basis(mean_x, mean_y, mean_z):
    inverse_norm = 1.0 / jnp.sqrt(mean_x * mean_x + mean_y * mean_y + mean_z * mean_z)
    unit_x = mean_x * inverse_norm
    unit_y = mean_y * inverse_norm
    unit_z = mean_z * inverse_norm
    square_x = unit_x * unit_x
    square_y = unit_y * unit_y
    square_z = unit_z * unit_z
    return [
        HARM_ZERO * jnp.ones_like(unit_x),
        -HARM_ONE * unit_y,
        HARM_ONE * unit_z,
        -HARM_ONE * unit_x,
        HARM_TWO[0] * unit_x * unit_y,
        HARM_TWO[1] * unit_y * unit_z,
        HARM_TWO[2] * (2.0 * square_z - square_x - square_y),
        HARM_TWO[3] * unit_x * unit_z,
        HARM_TWO[4] * (square_x - square_y),
        HARM_THREE[0] * unit_y * (3.0 * square_x - square_y),
        HARM_THREE[1] * unit_x * unit_y * unit_z,
        HARM_THREE[2] * unit_y * (4.0 * square_z - square_x - square_y),
        HARM_THREE[3] * unit_z * (2.0 * square_z - 3.0 * square_x - 3.0 * square_y),
        HARM_THREE[4] * unit_x * (4.0 * square_z - square_x - square_y),
        HARM_THREE[5] * unit_z * (square_x - square_y),
        HARM_THREE[6] * unit_x * (square_x - 3.0 * square_y),
    ]


def project(param):
    mean_x, mean_y, mean_z = param(0), param(1), param(2)
    scales = [jnp.exp(param(3 + axis)) for axis in range(3)]
    quat = [param(6 + part) for part in range(4)]
    quat_norm = jnp.sqrt(quat[0] * quat[0] + quat[1] * quat[1] + quat[2] * quat[2] + quat[3] * quat[3])
    quat_w, quat_x, quat_y, quat_z = (part / quat_norm for part in quat)
    rotation = [
        [
            1.0 - 2.0 * (quat_y * quat_y + quat_z * quat_z),
            2.0 * (quat_x * quat_y - quat_w * quat_z),
            2.0 * (quat_x * quat_z + quat_w * quat_y),
        ],
        [
            2.0 * (quat_x * quat_y + quat_w * quat_z),
            1.0 - 2.0 * (quat_x * quat_x + quat_z * quat_z),
            2.0 * (quat_y * quat_z - quat_w * quat_x),
        ],
        [
            2.0 * (quat_x * quat_z - quat_w * quat_y),
            2.0 * (quat_y * quat_z + quat_w * quat_x),
            1.0 - 2.0 * (quat_x * quat_x + quat_y * quat_y),
        ],
    ]
    scaled = [[rotation[row][col] * scales[col] for col in range(3)] for row in range(3)]
    sigma = [
        [sum(scaled[row][inner] * scaled[col][inner] for inner in range(3)) for col in range(3)]
        for row in range(3)
    ]
    inverse_depth = 1.0 / mean_z
    jac_diag = FOCAL_LENGTH * inverse_depth
    jac_first = -FOCAL_LENGTH * mean_x * inverse_depth * inverse_depth
    jac_second = -FOCAL_LENGTH * mean_y * inverse_depth * inverse_depth
    upper_row = [jac_diag * sigma[0][col] + jac_first * sigma[2][col] for col in range(3)]
    lower_row = [jac_diag * sigma[1][col] + jac_second * sigma[2][col] for col in range(3)]
    entry_a = upper_row[0] * jac_diag + upper_row[2] * jac_first + BLUR_TERM
    entry_b = upper_row[1] * jac_diag + upper_row[2] * jac_second
    entry_c = lower_row[1] * jac_diag + lower_row[2] * jac_second + BLUR_TERM
    determinant = entry_a * entry_c - entry_b * entry_b
    centre_u = FOCAL_LENGTH * mean_x * inverse_depth + CENTRE_SHIFT
    centre_v = FOCAL_LENGTH * mean_y * inverse_depth + CENTRE_SHIFT
    log_opacity = jnp.maximum(-jnp.log2(1.0 + jnp.exp(-param(10))), -10000.0)
    basis = sh_basis(mean_x, mean_y, mean_z)
    colour = [0.5 + sum(param(11 + 16 * c + k) * basis[k] for k in range(16)) for c in range(3)]
    attributes = [
        colour[0],
        colour[1],
        centre_u,
        centre_v,
        entry_c / determinant,
        -entry_b / determinant,
        entry_a / determinant,
        log_opacity,
        colour[2],
    ]
    kept = [jnp.where(value == value, jnp.clip(value, -1e30, 1e30), 0.0) for value in attributes]
    return kept, basis


def split_three(values):
    high = values.astype(BF16)
    rest = values - high.astype(F32)
    middle = rest.astype(BF16)
    low = (rest - middle.astype(F32)).astype(BF16)
    return high, middle, low


def split_two(values):
    high = values.astype(BF16)
    return high, (values - high.astype(F32)).astype(BF16)


def build_table(rows_ref, table_ref, ninth_ref, groups):
    for pair in range(groups // 2):
        part = []
        for q in (2 * pair, 2 * pair + 1):
            part.append(
                jnp.concatenate(
                    [rows_ref[pl.ds(18 * q, 8), :], rows_ref[pl.ds(18 * q + 9, 8), :]], axis=1
                )
            )
        pieces = split_three(jnp.concatenate(part, axis=0))
        for index, piece in enumerate(pieces):
            table_ref[pl.ds(16 * pair, 16), pl.ds(UNIT * index, UNIT)] = piece
    ninth = jnp.concatenate(
        [rows_ref[pl.ds(8, groups, stride=18), :], rows_ref[pl.ds(17, groups, stride=18), :]], axis=1
    )
    for index, piece in enumerate(split_two(ninth)):
        ninth_ref[:, pl.ds(UNIT * index, UNIT)] = piece


def one_hot(low_index):
    rows = lax.broadcasted_iota(jnp.int32, (UNIT, UNIT), 0)
    return jnp.where(rows == low_index, 1.0, 0.0).astype(BF16)


def gather_block(entries, table_ref, ninth_ref, groups):
    low_index = entries & (UNIT - 1)
    high_index = entries >> 8
    chosen = one_hot(low_index)
    tripled = jnp.concatenate([chosen, chosen, chosen], axis=0)
    every = jnp.dot(table_ref[...], tripled, preferred_element_type=F32)
    high_rows = jnp.broadcast_to(high_index, (8, UNIT))
    picked = jnp.zeros((8, UNIT), F32)
    for q in range(groups):
        picked = jnp.where(high_rows == q, every[8 * q : 8 * q + 8], picked)
    every_ninth = jnp.dot(ninth_ref[...], tripled[: 2 * UNIT], preferred_element_type=F32)
    group_rows = lax.broadcasted_iota(jnp.int32, (groups, UNIT), 0)
    ninth = jnp.sum(jnp.where(group_rows == high_index, every_ninth, 0.0), axis=0, keepdims=True)
    return picked, ninth


def scatter_terms(entries, values, groups):
    low_index = entries & (UNIT - 1)
    high_index = entries >> 8
    chosen = one_hot(low_index)
    group_rows = lax.broadcasted_iota(jnp.int32, (groups, UNIT), 0)
    member = group_rows == high_index
    highs, lows = [], []
    for c in range(3):
        value = jnp.where(member, values[c : c + 1], 0.0)
        high, low = split_two(value)
        highs.append(high)
        lows.append(low)
    left = jnp.concatenate([jnp.concatenate(highs, axis=0), jnp.concatenate(lows, axis=0)], axis=1)
    return left, jnp.concatenate([chosen, chosen], axis=1)


def dot_transposed(left, right):
    return lax.dot_general(left, right, (((1,), (1,)), ((), ())), preferred_element_type=F32)


OWN_UNROLL = 8


def own_kernel(gaussians, index_ref, send_ref, basis_ref, params, rows_ref, table_ref, ninth_ref, sems):
    def fetch(k):
        return pltpu.make_async_copy(
            gaussians.at[:, pl.ds(pl.multiple_of(k * LANES, LANES), LANES)],
            params.at[pl.ds(pl.multiple_of(k * PAD_PARAMS, PAD_PARAMS), PARAMS), :],
            sems.at[k],
        )

    def start(k, carry):
        fetch(k).start()
        return carry

    lax.fori_loop(0, OWNED // LANES, start, 0)

    def group(kb, carry):
        for k in range(8):
            fetch(8 * kb + k).wait()

        def param(a):
            return params[pl.ds(kb * 8 * PAD_PARAMS + a, 8, stride=PAD_PARAMS), :]

        attributes, basis = project(param)
        for a in range(ATTRS):
            rows_ref[pl.ds(kb * 8 * ATTRS + a, 8, stride=ATTRS), :] = attributes[a]
        for k in range(16):
            basis_ref[pl.ds(kb * 8 * 16 + k, 8, stride=16), :] = basis[k]
        return carry

    lax.fori_loop(0, OWNED // LANES // 8, group, 0)
    build_table(rows_ref, table_ref, ninth_ref, Q_OWN)

    def blocks(i, carry):
        index_rows = index_ref[pl.ds(pl.multiple_of(2 * OWN_UNROLL * i, 8), 2 * OWN_UNROLL), :]
        for j in range(OWN_UNROLL):
            entries = jnp.concatenate([index_rows[2 * j : 2 * j + 1], index_rows[2 * j + 1 : 2 * j + 2]], axis=1)
            picked, ninth = gather_block(entries, table_ref, ninth_ref, Q_OWN)
            for half in range(2):
                row = pl.multiple_of(i * (18 * OWN_UNROLL), 8) + 18 * j + 9 * half
                lanes = slice(LANES * half, LANES * half + LANES)
                send_ref[pl.ds(row, 8), :] = picked[:, lanes]
                send_ref[pl.ds(row + 8, 1), :] = ninth[:, lanes]
        return carry

    lax.fori_loop(0, PEERS // 2 // OWN_UNROLL, blocks, 0)


GATHER_UNROLL = 4
RENDER_UNROLL = 2
SCATTER_UNROLL = 4
MOST = TILE_DEV * BLOCKS
LISTED = MOST + 8


def render_kernel(
    received,
    slots_ref,
    cot_ref,
    counts_ref,
    rank_ref,
    image_ref,
    grad_ref,
    table_ref,
    ninth_ref,
    triangle_ref,
    entries_ref,
    attr_ref,
    attr_ninth_ref,
    value_ref,
    total_ref,
    picture_ref,
    listed,
):
    build_table(received, table_ref, ninth_ref, Q_SLOT)
    before = lax.broadcasted_iota(jnp.int32, (UNIT, UNIT), 0)
    after = lax.broadcasted_iota(jnp.int32, (UNIT, UNIT), 1)
    triangle = jnp.where(before < after, 1.0, 0.0).astype(BF16)
    triangle_ref[pl.ds(0, UNIT), :] = triangle
    triangle_ref[pl.ds(UNIT, UNIT), :] = triangle
    picture_ref[...] = jnp.zeros_like(picture_ref)
    total_ref[...] = jnp.zeros_like(total_ref)

    def list_tile(t, n):
        count = counts_ref[t]

        def list_block(b, n):
            listed[n] = t * 8 + b
            entries_ref[n] = slots_ref[t, pl.ds(b, 1), :]
            return n + 1

        return lax.fori_loop(0, count, list_block, n)

    live = lax.fori_loop(0, TILE_DEV, list_tile, 0)
    for extra in range(8):
        listed[live + extra] = TILE_DEV * 8
        entries_ref[live + extra] = jnp.zeros((1, UNIT), jnp.int32)

    def gather_step(i, carry):
        for j in range(GATHER_UNROLL):
            n = i * GATHER_UNROLL + j
            picked, ninth = gather_block(entries_ref[n], table_ref, ninth_ref, Q_SLOT)
            attr_ref[n] = picked
            attr_ninth_ref[n] = ninth
        return carry

    lax.fori_loop(0, (live + GATHER_UNROLL - 1) // GATHER_UNROLL, gather_step, 0)

    rank = rank_ref[0]
    lane_ones = jnp.ones((1, UNIT), F32)
    lane_zeros = jnp.zeros((4, UNIT), F32)
    across = lax.broadcasted_iota(jnp.int32, (8, UNIT), 0)

    def render_one(n, trans):
        code = listed[n]
        t = code >> 3
        first = (code & 7) == 0
        local_tile = (rank * TILE_DEV + t) % 256
        origin_x = (16 * (local_tile % 16)).astype(F32) + 0.5
        origin_y = (16 * (local_tile // 16)).astype(F32) + 0.5
        picked = attr_ref[n]

        def wide(row):
            return jnp.broadcast_to(picked[row : row + 1], (8, UNIT))

        centre_u, centre_v = wide(2), wide(3)
        form_a = wide(4) * (-0.5 * LOG2E)
        form_b = wide(5) * (-LOG2E)
        form_c = wide(6) * (-0.5 * LOG2E)
        log_opacity = wide(7)
        constant, linear = [], []
        for half in range(2):
            delta_x = (across.astype(F32) + (origin_x + 8.0 * half)) - centre_u
            constant.append(form_a * delta_x * delta_x + log_opacity)
            linear.append(form_b * delta_x)
        powers = []
        for y in range(16):
            delta_y = (origin_y + y) - centre_v
            bent = form_c * delta_y
            for half in range(2):
                powers.append(constant[half] + delta_y * (linear[half] + bent))
        alpha = jnp.exp2(jnp.concatenate(powers, axis=0))
        log_keep = jnp.log2(1.0 - alpha)
        kept_high, kept_low = split_two(log_keep)
        earlier = jnp.dot(
            jnp.concatenate([kept_high, kept_low], axis=1), triangle_ref[...], preferred_element_type=F32
        )
        weight = alpha * jnp.exp2(earlier)
        weight_high, weight_low = split_two(weight)
        columns = jnp.concatenate([picked[0:2], attr_ninth_ref[n], lane_ones, lane_zeros], axis=0)
        colour_high, colour_low = split_two(columns)
        nothing = jnp.zeros((8, UNIT), BF16)
        left = jnp.concatenate(
            [
                jnp.concatenate([colour_high, colour_low], axis=0),
                jnp.concatenate([colour_high, nothing], axis=0),
            ],
            axis=1,
        )
        seen = dot_transposed(left, jnp.concatenate([weight_high, weight_low], axis=1))
        seen = seen[:8] + seen[8:]
        trans = jnp.where(first, jnp.ones_like(trans), trans)
        shown = seen * trans
        cot = jnp.concatenate([cot_ref[0, pl.ds(jnp.minimum(t, TILE_DEV - 1), 1), :],
                               cot_ref[1, pl.ds(jnp.minimum(t, TILE_DEV - 1), 1), :],
                               cot_ref[2, pl.ds(jnp.minimum(t, TILE_DEV - 1), 1), :],
                               lane_ones, lane_zeros], axis=0)
        cot_high, cot_low = split_two(cot * trans)
        left = jnp.concatenate(
            [
                jnp.concatenate([cot_high, cot_low], axis=0),
                jnp.concatenate([cot_high, nothing], axis=0),
            ],
            axis=1,
        )
        back = jnp.dot(
            left, jnp.concatenate([weight_high, weight_low], axis=0), preferred_element_type=F32
        )
        back = back[:8] + back[8:]
        value_ref[n] = jnp.where(t < TILE_DEV, back, 0.0)
        picture_ref[t] = jnp.where(first, shown, picture_ref[t] + shown)
        return jnp.maximum(trans * (1.0 - seen[3:4]), 0.0)

    def render_step(i, trans):
        for j in range(RENDER_UNROLL):
            trans = render_one(i * RENDER_UNROLL + j, trans)
        return trans

    lax.fori_loop(0, (live + RENDER_UNROLL - 1) // RENDER_UNROLL, render_step, jnp.ones((1, UNIT), F32))
    for extra in range(8):
        value_ref[live + extra] = jnp.zeros((8, UNIT), F32)

    def scatter_step(i, carry):
        lefts, rights = [], []
        for j in range(SCATTER_UNROLL):
            n = i * SCATTER_UNROLL + j
            left, right = scatter_terms(entries_ref[n], value_ref[n], Q_SLOT)
            lefts.append(left)
            rights.append(right)
        total_ref[...] += dot_transposed(jnp.concatenate(lefts, axis=1), jnp.concatenate(rights, axis=1))
        return carry

    lax.fori_loop(0, (live + SCATTER_UNROLL - 1) // SCATTER_UNROLL, scatter_step, 0)
    for c in range(3):
        for half in range(2):
            grad_ref[pl.ds(3 * half + c, Q_SLOT, stride=6), :] = total_ref[
                pl.ds(c * Q_SLOT, Q_SLOT), pl.ds(half * LANES, LANES)
            ]
    for t in range(TILE_DEV):
        for c in range(3):
            image_ref[c, pl.ds(t, 1), :] = picture_ref[t, pl.ds(c, 1), :]


FINISH_UNROLL = 4


def finish_kernel(returned, index_ref, basis_ref, out_ref, total_ref):
    total_ref[...] = jnp.zeros_like(total_ref)

    def scatter_step(i, carry):
        rows = returned[pl.ds(pl.multiple_of(i * (6 * FINISH_UNROLL), 8), 6 * FINISH_UNROLL), :]
        index_rows = index_ref[pl.ds(pl.multiple_of(2 * FINISH_UNROLL * i, 8), 2 * FINISH_UNROLL), :]
        lefts, rights = [], []
        for j in range(FINISH_UNROLL):
            entries = jnp.concatenate([index_rows[2 * j : 2 * j + 1], index_rows[2 * j + 1 : 2 * j + 2]], axis=1)
            values = jnp.concatenate([rows[6 * j : 6 * j + 3], rows[6 * j + 3 : 6 * j + 6]], axis=1)
            left, right = scatter_terms(entries, values, Q_OWN)
            lefts.append(left)
            rights.append(right)
        total_ref[...] += dot_transposed(jnp.concatenate(lefts, axis=1), jnp.concatenate(rights, axis=1))
        return carry

    lax.fori_loop(0, PEERS // 2 // FINISH_UNROLL, scatter_step, 0)
    for k in range(OWNED // LANES):
        basis = basis_ref[pl.ds(16 * k, 16), :]
        for c in range(3):
            grad = total_ref[pl.ds(c * Q_OWN + k // 2, 1), pl.ds((k % 2) * LANES, LANES)]
            out_ref[pl.ds(16 * c, 16), pl.ds(k * LANES, LANES)] = basis * grad


def exchange(buffer):
    return lax.all_to_all(buffer, AXES, split_axis=0, concat_axis=0, tiled=True)


def per_device(gaussians, send_index, tile_slots, block_count, cotangent):
    vmem = pl.BlockSpec(memory_space=pltpu.VMEM)
    smem = pl.BlockSpec(memory_space=pltpu.SMEM)
    limits = pltpu.CompilerParams(vmem_limit_bytes=VMEM_BYTES)
    shape = jax.ShapeDtypeStruct
    rank = lax.axis_index(AXES).astype(jnp.int32).reshape(1)
    index = send_index.reshape(PEERS, WIDTH)
    send, basis = pl.pallas_call(
        own_kernel,
        out_shape=(shape((ATTRS * PEERS, WIDTH), F32), shape((16 * OWNED // LANES, LANES), F32)),
        in_specs=[pl.BlockSpec(memory_space=pl.ANY), vmem],
        out_specs=(vmem, vmem),
        scratch_shapes=[
            pltpu.VMEM((PAD_PARAMS * OWNED // LANES, LANES), F32),
            pltpu.VMEM((ATTRS * OWNED // LANES, LANES), F32),
            pltpu.VMEM((8 * Q_OWN, 3 * UNIT), BF16),
            pltpu.VMEM((Q_OWN, 2 * UNIT), BF16),
            pltpu.SemaphoreType.DMA((OWNED // LANES,)),
        ],
        compiler_params=limits,
        name="project_and_pack",
    )(gaussians, index)
    received = exchange(send.reshape(PEERS, ATTRS * WIDTH)).reshape(ATTRS * PEERS, WIDTH)
    image, slot_grad = pl.pallas_call(
        render_kernel,
        out_shape=(shape((3, TILE_DEV, UNIT), F32), shape((3 * PEERS, WIDTH), F32)),
        in_specs=[vmem, vmem, vmem, smem, smem],
        out_specs=(vmem, vmem),
        scratch_shapes=[
            pltpu.VMEM((8 * Q_SLOT, 3 * UNIT), BF16),
            pltpu.VMEM((Q_SLOT, 2 * UNIT), BF16),
            pltpu.VMEM((2 * UNIT, UNIT), BF16),
            pltpu.VMEM((LISTED, 1, UNIT), jnp.int32),
            pltpu.VMEM((LISTED, 8, UNIT), F32),
            pltpu.VMEM((LISTED, 1, UNIT), F32),
            pltpu.VMEM((LISTED, 8, UNIT), F32),
            pltpu.VMEM((3 * Q_SLOT, UNIT), F32),
            pltpu.VMEM((TILE_DEV + 1, 8, UNIT), F32),
            pltpu.SMEM((LISTED,), jnp.int32),
        ],
        compiler_params=limits,
        name="render",
    )(received, tile_slots, cotangent, block_count, rank)
    returned = exchange(slot_grad.reshape(PEERS, 3 * WIDTH)).reshape(3 * PEERS, WIDTH)
    sh_grad = pl.pallas_call(
        finish_kernel,
        out_shape=shape((48, OWNED), F32),
        in_specs=[vmem, vmem, vmem],
        out_specs=vmem,
        scratch_shapes=[pltpu.VMEM((3 * Q_OWN, UNIT), F32)],
        compiler_params=limits,
        name="finish",
    )(returned, index, basis)
    return image, sh_grad


def solution(mesh):
    placed = (
        P(None, AXES),
        P(AXES, None, None),
        P(AXES, None, None),
        P(AXES),
        P(None, AXES, None),
    )
    return jax.shard_map(
        per_device,
        mesh=mesh,
        in_specs=placed,
        out_specs=(P(None, AXES, None), P(None, AXES)),
        check_vma=False,
    )
```

```python
import jax
import jax.numpy as jnp
from jax import lax
from jax.experimental import pallas as pl
from jax.experimental.pallas import tpu as pltpu
from jax.sharding import PartitionSpec as P

AXES = ("cell", "tile")
PEERS = 128
WIDTH = 128
OWNED = 8192
SLOTS = 16384
TILE_DEV = 32
BLOCKS = 4
PARAMS = 59
ATTRS = 9
UNIT = 256
Q_OWN = OWNED // UNIT
Q_SLOT = SLOTS // UNIT
LANES = 128
PAD_PARAMS = 64
F32 = jnp.float32
BF16 = jnp.bfloat16
VMEM_BYTES = 48 * 2**20

FOCAL_LENGTH = 256.0
CENTRE_SHIFT = 128.0
BLUR_TERM = 0.3
LOG2E = 1.4426950408889634
HARM_ZERO = 0.28209479177387814
HARM_ONE = 0.4886025119029199
HARM_TWO = (
    1.0925484305920792,
    -1.0925484305920792,
    0.31539156525252005,
    -1.0925484305920792,
    0.5462742152960396,
)
HARM_THREE = (
    -0.5900435899266435,
    2.890611442640554,
    -0.4570457994644658,
    0.3731763325901154,
    -0.4570457994644658,
    1.445305721320277,
    -0.5900435899266435,
)


def sh_basis(mean_x, mean_y, mean_z):
    inverse_norm = 1.0 / jnp.sqrt(mean_x * mean_x + mean_y * mean_y + mean_z * mean_z)
    unit_x = mean_x * inverse_norm
    unit_y = mean_y * inverse_norm
    unit_z = mean_z * inverse_norm
    square_x = unit_x * unit_x
    square_y = unit_y * unit_y
    square_z = unit_z * unit_z
    return [
        HARM_ZERO * jnp.ones_like(unit_x),
        -HARM_ONE * unit_y,
        HARM_ONE * unit_z,
        -HARM_ONE * unit_x,
        HARM_TWO[0] * unit_x * unit_y,
        HARM_TWO[1] * unit_y * unit_z,
        HARM_TWO[2] * (2.0 * square_z - square_x - square_y),
        HARM_TWO[3] * unit_x * unit_z,
        HARM_TWO[4] * (square_x - square_y),
        HARM_THREE[0] * unit_y * (3.0 * square_x - square_y),
        HARM_THREE[1] * unit_x * unit_y * unit_z,
        HARM_THREE[2] * unit_y * (4.0 * square_z - square_x - square_y),
        HARM_THREE[3] * unit_z * (2.0 * square_z - 3.0 * square_x - 3.0 * square_y),
        HARM_THREE[4] * unit_x * (4.0 * square_z - square_x - square_y),
        HARM_THREE[5] * unit_z * (square_x - square_y),
        HARM_THREE[6] * unit_x * (square_x - 3.0 * square_y),
    ]


def project(param):
    mean_x, mean_y, mean_z = param(0), param(1), param(2)
    scales = [jnp.exp(param(3 + axis)) for axis in range(3)]
    quat = [param(6 + part) for part in range(4)]
    quat_norm = jnp.sqrt(quat[0] * quat[0] + quat[1] * quat[1] + quat[2] * quat[2] + quat[3] * quat[3])
    quat_w, quat_x, quat_y, quat_z = (part / quat_norm for part in quat)
    rotation = [
        [
            1.0 - 2.0 * (quat_y * quat_y + quat_z * quat_z),
            2.0 * (quat_x * quat_y - quat_w * quat_z),
            2.0 * (quat_x * quat_z + quat_w * quat_y),
        ],
        [
            2.0 * (quat_x * quat_y + quat_w * quat_z),
            1.0 - 2.0 * (quat_x * quat_x + quat_z * quat_z),
            2.0 * (quat_y * quat_z - quat_w * quat_x),
        ],
        [
            2.0 * (quat_x * quat_z - quat_w * quat_y),
            2.0 * (quat_y * quat_z + quat_w * quat_x),
            1.0 - 2.0 * (quat_x * quat_x + quat_y * quat_y),
        ],
    ]
    scaled = [[rotation[row][col] * scales[col] for col in range(3)] for row in range(3)]
    sigma = [
        [sum(scaled[row][inner] * scaled[col][inner] for inner in range(3)) for col in range(3)]
        for row in range(3)
    ]
    inverse_depth = 1.0 / mean_z
    jac_diag = FOCAL_LENGTH * inverse_depth
    jac_first = -FOCAL_LENGTH * mean_x * inverse_depth * inverse_depth
    jac_second = -FOCAL_LENGTH * mean_y * inverse_depth * inverse_depth
    upper_row = [jac_diag * sigma[0][col] + jac_first * sigma[2][col] for col in range(3)]
    lower_row = [jac_diag * sigma[1][col] + jac_second * sigma[2][col] for col in range(3)]
    entry_a = upper_row[0] * jac_diag + upper_row[2] * jac_first + BLUR_TERM
    entry_b = upper_row[1] * jac_diag + upper_row[2] * jac_second
    entry_c = lower_row[1] * jac_diag + lower_row[2] * jac_second + BLUR_TERM
    determinant = entry_a * entry_c - entry_b * entry_b
    centre_u = FOCAL_LENGTH * mean_x * inverse_depth + CENTRE_SHIFT
    centre_v = FOCAL_LENGTH * mean_y * inverse_depth + CENTRE_SHIFT
    log_opacity = jnp.maximum(-jnp.log2(1.0 + jnp.exp(-param(10))), -10000.0)
    basis = sh_basis(mean_x, mean_y, mean_z)
    colour = [0.5 + sum(param(11 + 16 * c + k) * basis[k] for k in range(16)) for c in range(3)]
    attributes = [
        colour[0],
        colour[1],
        centre_u,
        centre_v,
        entry_c / determinant,
        -entry_b / determinant,
        entry_a / determinant,
        log_opacity,
        colour[2],
    ]
    kept = [jnp.where(value == value, jnp.clip(value, -1e30, 1e30), 0.0) for value in attributes]
    return kept, basis


def split_three(values):
    high = values.astype(BF16)
    rest = values - high.astype(F32)
    middle = rest.astype(BF16)
    low = (rest - middle.astype(F32)).astype(BF16)
    return high, middle, low


def split_two(values):
    high = values.astype(BF16)
    return high, (values - high.astype(F32)).astype(BF16)


def build_table(rows_ref, table_ref, groups):
    inner = lax.broadcasted_iota(jnp.int32, (16, UNIT), 0) & 7
    for pair in range(groups // 2):
        part, ninth = [], []
        for q in (2 * pair, 2 * pair + 1):
            halves = [rows_ref[pl.ds(18 * q, 8), :], rows_ref[pl.ds(18 * q + 9, 8), :]]
            part.append(jnp.concatenate(halves, axis=1))
            halves = [rows_ref[pl.ds(18 * q + 8, 1), :], rows_ref[pl.ds(18 * q + 17, 1), :]]
            ninth.append(jnp.broadcast_to(jnp.concatenate(halves, axis=1), (8, UNIT)))
        first, second, third = split_three(jnp.concatenate(part, axis=0))
        high, low = split_two(jnp.concatenate(ninth, axis=0))
        tail = jnp.where(
            inner == 0, high.astype(F32), jnp.where(inner == 1, low.astype(F32), third.astype(F32))
        ).astype(BF16)
        for index, piece in enumerate((first, second, tail)):
            table_ref[pl.ds(8 * groups * index + 16 * pair, 16), :] = piece


def one_hot(low_index):
    rows = lax.broadcasted_iota(jnp.int32, (UNIT, UNIT), 0)
    return jnp.where(rows == low_index, 1.0, 0.0).astype(BF16)


def gather_block(entries, table_ref, groups):
    every = jnp.dot(table_ref[...], one_hot(entries & (UNIT - 1)), preferred_element_type=F32)
    high_rows = jnp.broadcast_to(entries >> 8, (8, UNIT))
    picked = [jnp.zeros((8, UNIT), F32)] * 3
    for q in range(groups):
        member = high_rows == q
        for index in range(3):
            start = 8 * groups * index + 8 * q
            picked[index] = jnp.where(member, every[start : start + 8], picked[index])
    inner = lax.broadcasted_iota(jnp.int32, (8, UNIT), 0)
    tail = picked[2]
    return picked[0] + (picked[1] + jnp.where(inner < 2, 0.0, tail)), tail[0:1] + tail[1:2]


def scatter_terms(entries, values, groups):
    chosen = one_hot(entries & (UNIT - 1))
    group_rows = lax.broadcasted_iota(jnp.int32, (groups, UNIT), 0)
    member = jnp.where(group_rows == (entries >> 8), 1.0, 0.0).astype(BF16)
    high, low = split_two(values)
    rows = [member * part[c : c + 1] for part in (high, low) for c in range(3)]
    return jnp.concatenate(rows, axis=0), chosen


def dot_transposed(left, right):
    return lax.dot_general(left, right, (((1,), (1,)), ((), ())), preferred_element_type=F32)


OWN_UNROLL = 32


def own_kernel(gaussians, index_hbm, send_ref, basis_ref, params, rows_ref, table_ref, index_ref, sems, index_sem):
    def fetch(k):
        return pltpu.make_async_copy(
            gaussians.at[:, pl.ds(pl.multiple_of(k * LANES, LANES), LANES)],
            params.at[pl.ds(pl.multiple_of(k * PAD_PARAMS, PAD_PARAMS), PARAMS), :],
            sems.at[k],
        )

    def start(k, carry):
        fetch(k).start()
        return carry

    lax.fori_loop(0, OWNED // LANES, start, 0)
    index_copy = pltpu.make_async_copy(index_hbm, index_ref, index_sem)
    index_copy.start()

    def group(kb, carry):
        for k in range(8):
            fetch(8 * kb + k).wait()

        def param(a):
            return params[pl.ds(kb * 8 * PAD_PARAMS + a, 8, stride=PAD_PARAMS), :]

        attributes, basis = project(param)
        for a in range(ATTRS):
            rows_ref[pl.ds(kb * 8 * ATTRS + a, 8, stride=ATTRS), :] = attributes[a]
        for k in range(16):
            basis_ref[pl.ds(kb * 8 * 16 + k, 8, stride=16), :] = basis[k]
        return carry

    lax.fori_loop(0, OWNED // LANES // 8, group, 0)
    build_table(rows_ref, table_ref, Q_OWN)
    index_copy.wait()

    def blocks(i, carry):
        index_rows = index_ref[pl.ds(pl.multiple_of(2 * OWN_UNROLL * i, 8), 2 * OWN_UNROLL), :]
        for j in range(OWN_UNROLL):
            entries = jnp.concatenate([index_rows[2 * j : 2 * j + 1], index_rows[2 * j + 1 : 2 * j + 2]], axis=1)
            picked, ninth = gather_block(entries, table_ref, Q_OWN)
            for half in range(2):
                row = pl.multiple_of(i * (18 * OWN_UNROLL), 8) + 18 * j + 9 * half
                lanes = slice(LANES * half, LANES * half + LANES)
                send_ref[pl.ds(row, 8), :] = picked[:, lanes]
                send_ref[pl.ds(row + 8, 1), :] = ninth[:, lanes]
        return carry

    lax.fori_loop(0, PEERS // 2 // OWN_UNROLL, blocks, 0)


GATHER_UNROLL = 8
RENDER_UNROLL = 4
MOST = TILE_DEV * BLOCKS
LISTED = MOST + 8


def render_kernel(
    received,
    slots_ref,
    cot_ref,
    counts_ref,
    rank_ref,
    image_ref,
    grad_ref,
    table_ref,
    triangle_ref,
    entries_ref,
    attr_ref,
    attr_ninth_ref,
    gone_ref,
    total_ref,
    picture_ref,
    listed,
):
    build_table(received, table_ref, Q_SLOT)
    before = lax.broadcasted_iota(jnp.int32, (UNIT, UNIT), 0)
    after = lax.broadcasted_iota(jnp.int32, (UNIT, UNIT), 1)
    triangle = jnp.where(before < after, 1.0, 0.0).astype(BF16)
    triangle_ref[...] = triangle
    picture_ref[...] = jnp.zeros_like(picture_ref)
    total_ref[...] = jnp.zeros_like(total_ref)

    def list_tile(t, n):
        count = counts_ref[t]

        def list_block(b, n):
            listed[n] = t * 8 + b
            entries_ref[n] = slots_ref[t, pl.ds(b, 1), :]
            return n + 1

        return lax.fori_loop(0, count, list_block, n)

    live = lax.fori_loop(0, TILE_DEV, list_tile, 0)
    for extra in range(8):
        listed[live + extra] = TILE_DEV * 8
        entries_ref[live + extra] = jnp.zeros((1, UNIT), jnp.int32)

    def gather_step(i, carry):
        for j in range(GATHER_UNROLL):
            n = i * GATHER_UNROLL + j
            picked, ninth = gather_block(entries_ref[n], table_ref, Q_SLOT)
            attr_ref[n] = picked
            attr_ninth_ref[n] = ninth
        return carry

    lax.fori_loop(0, (live + GATHER_UNROLL - 1) // GATHER_UNROLL, gather_step, 0)

    rank = rank_ref[0]
    lane_ones = jnp.zeros((5, UNIT), F32)
    across = lax.broadcasted_iota(jnp.int32, (8, UNIT), 0).astype(F32)

    def render_one(n):
        code = listed[n]
        t = code >> 3
        source = jnp.minimum(t, TILE_DEV - 1)
        first = (code & 7) == 0
        local_tile = (rank * TILE_DEV + t) % 256
        origin_x = (16 * (local_tile % 16)).astype(F32) + 0.5
        origin_y = (16 * (local_tile // 16)).astype(F32) + 0.5
        picked = attr_ref[n]

        def wide(row):
            return jnp.broadcast_to(picked[row : row + 1], (8, UNIT))

        centre_u, centre_v = wide(2), wide(3)
        form_a = wide(4) * (-0.5 * LOG2E)
        form_b = wide(5) * (-LOG2E)
        form_c = wide(6) * (-0.5 * LOG2E)
        log_opacity = wide(7)
        constant, linear = [], []
        for half in range(2):
            delta_x = (across + (origin_x + 8.0 * half)) - centre_u
            constant.append(form_a * delta_x * delta_x + log_opacity)
            linear.append(form_b * delta_x)
        powers = []
        for y in range(16):
            delta_y = (origin_y + y) - centre_v
            bent = form_c * delta_y
            for half in range(2):
                powers.append(constant[half] + delta_y * (linear[half] + bent))
        alpha = jnp.exp2(jnp.concatenate(powers, axis=0))
        log_keep = jnp.log2(1.0 - alpha)
        sums = jnp.dot(jnp.concatenate(split_two(log_keep), axis=0), triangle_ref[...], preferred_element_type=F32)
        cot = jnp.concatenate([cot_ref[c, pl.ds(source, 1), :] for c in range(3)] + [lane_ones], axis=0)
        cot_columns = jnp.transpose(cot)
        kept = jnp.where(first, 0.0, 1.0)
        back = [[jnp.zeros((8, LANES), F32) for half in range(2)] for c in range(3)]
        weights = []
        for p in range(UNIT // 8):
            rows = slice(8 * p, 8 * p + 8)
            gone = gone_ref[pl.ds(8 * p, 8), :] * kept
            earlier = (sums[rows] + sums[UNIT + 8 * p : UNIT + 8 * p + 8]) + jnp.concatenate([gone, gone], axis=1)
            weight = alpha[rows] * jnp.exp2(earlier)
            last = (earlier + log_keep[rows])[:, UNIT - 1 : UNIT]
            gone_ref[pl.ds(8 * p, 8), :] = jnp.broadcast_to(last, (8, LANES))
            for c in range(3):
                column = jnp.broadcast_to(cot_columns[rows, c : c + 1], (8, LANES))
                for half in range(2):
                    back[c][half] += column * weight[:, LANES * half : LANES * half + LANES]
            weights.append(weight)
        weight_high, weight_low = split_two(jnp.concatenate(weights, axis=0))
        columns = jnp.concatenate([picked[0:2], attr_ninth_ref[n], lane_ones], axis=0)
        colour_high, colour_low = split_two(columns)
        nothing = jnp.zeros((8, UNIT), BF16)
        left = jnp.concatenate(
            [
                jnp.concatenate([colour_high, colour_low], axis=0),
                jnp.concatenate([colour_high, nothing], axis=0),
            ],
            axis=1,
        )
        seen = dot_transposed(left, jnp.concatenate([weight_high, weight_low], axis=1))
        seen = seen[:8] + seen[8:]
        picture_ref[t] = jnp.where(first, seen, picture_ref[t] + seen)
        sums_back = [
            jnp.sum(jnp.concatenate(back[c], axis=1), axis=0, keepdims=True) for c in range(3)
        ]
        return jnp.where(t < TILE_DEV, jnp.concatenate(sums_back, axis=0), 0.0)

    def scatter_pair(n, values):
        lefts, rights = [], []
        for j in range(RENDER_UNROLL):
            left, right = scatter_terms(entries_ref[n + j], values[j], Q_SLOT)
            lefts.append(left)
            rights.append(right)
        total_ref[...] += dot_transposed(jnp.concatenate(lefts, axis=1), jnp.concatenate(rights, axis=1))

    def render_step(i, values):
        n = i * RENDER_UNROLL
        scatter_pair(jnp.maximum(n - RENDER_UNROLL, 0), values)
        return tuple(render_one(n + j) for j in range(RENDER_UNROLL))

    gone_ref[...] = jnp.zeros_like(gone_ref)
    steps = (live + RENDER_UNROLL - 1) // RENDER_UNROLL
    nothing_back = tuple(jnp.zeros((3, UNIT), F32) for j in range(RENDER_UNROLL))
    values = lax.fori_loop(0, steps, render_step, nothing_back)
    scatter_pair((steps - 1) * RENDER_UNROLL, values)
    for c in range(3):
        for half in range(2):
            lanes = pl.ds(half * LANES, LANES)
            grad_ref[pl.ds(3 * half + c, Q_SLOT, stride=6), :] = (
                total_ref[pl.ds(c * Q_SLOT, Q_SLOT), lanes]
                + total_ref[pl.ds((3 + c) * Q_SLOT, Q_SLOT), lanes]
            )
    for t in range(TILE_DEV):
        for c in range(3):
            image_ref[c, pl.ds(t, 1), :] = picture_ref[t, pl.ds(c, 1), :]


FINISH_UNROLL = 32


def finish_kernel(returned, index_ref, basis_ref, out_ref, total_ref):
    total_ref[...] = jnp.zeros_like(total_ref)

    def scatter_step(i, carry):
        rows = returned[pl.ds(pl.multiple_of(i * (6 * FINISH_UNROLL), 8), 6 * FINISH_UNROLL), :]
        index_rows = index_ref[pl.ds(pl.multiple_of(2 * FINISH_UNROLL * i, 8), 2 * FINISH_UNROLL), :]
        lefts, rights = [], []
        for j in range(FINISH_UNROLL):
            entries = jnp.concatenate([index_rows[2 * j : 2 * j + 1], index_rows[2 * j + 1 : 2 * j + 2]], axis=1)
            values = jnp.concatenate([rows[6 * j : 6 * j + 3], rows[6 * j + 3 : 6 * j + 6]], axis=1)
            left, right = scatter_terms(entries, values, Q_OWN)
            lefts.append(left)
            rights.append(right)
        total_ref[...] += dot_transposed(jnp.concatenate(lefts, axis=1), jnp.concatenate(rights, axis=1))
        return carry

    lax.fori_loop(0, PEERS // 2 // FINISH_UNROLL, scatter_step, 0)
    for k in range(OWNED // LANES):
        basis = basis_ref[pl.ds(16 * k, 16), :]
        for c in range(3):
            lanes = pl.ds((k % 2) * LANES, LANES)
            grad = (
                total_ref[pl.ds(c * Q_OWN + k // 2, 1), lanes]
                + total_ref[pl.ds((3 + c) * Q_OWN + k // 2, 1), lanes]
            )
            out_ref[pl.ds(16 * c, 16), pl.ds(k * LANES, LANES)] = basis * grad


def exchange(buffer):
    return lax.all_to_all(buffer, AXES, split_axis=0, concat_axis=0, tiled=True)


def per_device(gaussians, send_index, tile_slots, block_count, cotangent):
    vmem = pl.BlockSpec(memory_space=pltpu.VMEM)
    smem = pl.BlockSpec(memory_space=pltpu.SMEM)
    limits = pltpu.CompilerParams(vmem_limit_bytes=VMEM_BYTES)
    shape = jax.ShapeDtypeStruct
    rank = lax.axis_index(AXES).astype(jnp.int32).reshape(1)
    index = send_index.reshape(PEERS, WIDTH)
    send, basis = pl.pallas_call(
        own_kernel,
        out_shape=(shape((ATTRS * PEERS, WIDTH), F32), shape((16 * OWNED // LANES, LANES), F32)),
        in_specs=[pl.BlockSpec(memory_space=pltpu.HBM), pl.BlockSpec(memory_space=pltpu.HBM)],
        out_specs=(vmem, vmem),
        scratch_shapes=[
            pltpu.VMEM((PAD_PARAMS * OWNED // LANES, LANES), F32),
            pltpu.VMEM((ATTRS * OWNED // LANES, LANES), F32),
            pltpu.VMEM((24 * Q_OWN, UNIT), BF16),
            pltpu.VMEM((PEERS, WIDTH), jnp.int32),
            pltpu.SemaphoreType.DMA((OWNED // LANES,)),
            pltpu.SemaphoreType.DMA(()),
        ],
        compiler_params=pltpu.CompilerParams(vmem_limit_bytes=62 * 2**20),
        name="project_and_pack",
    )(gaussians, index)
    received = exchange(send.reshape(PEERS, ATTRS * WIDTH)).reshape(ATTRS * PEERS, WIDTH)
    image, slot_grad = pl.pallas_call(
        render_kernel,
        out_shape=(shape((3, TILE_DEV, UNIT), F32), shape((3 * PEERS, WIDTH), F32)),
        in_specs=[vmem, vmem, vmem, smem, smem],
        out_specs=(vmem, vmem),
        scratch_shapes=[
            pltpu.VMEM((24 * Q_SLOT, UNIT), BF16),
            pltpu.VMEM((UNIT, UNIT), BF16),
            pltpu.VMEM((LISTED, 1, UNIT), jnp.int32),
            pltpu.VMEM((LISTED, 8, UNIT), F32),
            pltpu.VMEM((LISTED, 1, UNIT), F32),
            pltpu.VMEM((UNIT, LANES), F32),
            pltpu.VMEM((6 * Q_SLOT, UNIT), F32),
            pltpu.VMEM((TILE_DEV + 1, 8, UNIT), F32),
            pltpu.SMEM((LISTED,), jnp.int32),
        ],
        compiler_params=limits,
        name="render",
    )(received, tile_slots, cotangent, block_count, rank)
    returned = exchange(slot_grad.reshape(PEERS, 3 * WIDTH)).reshape(3 * PEERS, WIDTH)
    sh_grad = pl.pallas_call(
        finish_kernel,
        out_shape=shape((48, OWNED), F32),
        in_specs=[vmem, vmem, vmem],
        out_specs=vmem,
        scratch_shapes=[pltpu.VMEM((6 * Q_OWN, UNIT), F32)],
        compiler_params=limits,
        name="finish",
    )(returned, index, basis)
    return image, sh_grad


def solution(mesh):
    placed = (
        P(None, AXES),
        P(AXES, None, None),
        P(AXES, None, None),
        P(AXES),
        P(None, AXES, None),
    )
    return jax.shard_map(
        per_device,
        mesh=mesh,
        in_specs=placed,
        out_specs=(P(None, AXES, None), P(None, AXES)),
        check_vma=False,
    )
```

```python
import jax
import jax.numpy as jnp
from jax import lax
from jax.experimental import pallas as pl
from jax.experimental.pallas import tpu as pltpu
from jax.sharding import PartitionSpec as P

AXES = ("cell", "tile")
PEERS = 128
WIDTH = 128
OWNED = 8192
SLOTS = 16384
TILE_DEV = 32
BLOCKS = 4
PARAMS = 59
ATTRS = 9
UNIT = 256
FORM = (5, 6, 7)
Q_OWN = OWNED // UNIT
Q_SLOT = SLOTS // UNIT
LANES = 128
PAD_PARAMS = 64
F32 = jnp.float32
BF16 = jnp.bfloat16
VMEM_BYTES = 48 * 2**20

FOCAL_LENGTH = 256.0
CENTRE_SHIFT = 128.0
BLUR_TERM = 0.3
LOG2E = 1.4426950408889634
HARM_ZERO = 0.28209479177387814
HARM_ONE = 0.4886025119029199
HARM_TWO = (
    1.0925484305920792,
    -1.0925484305920792,
    0.31539156525252005,
    -1.0925484305920792,
    0.5462742152960396,
)
HARM_THREE = (
    -0.5900435899266435,
    2.890611442640554,
    -0.4570457994644658,
    0.3731763325901154,
    -0.4570457994644658,
    1.445305721320277,
    -0.5900435899266435,
)


def sh_basis(mean_x, mean_y, mean_z):
    inverse_norm = 1.0 / jnp.sqrt(mean_x * mean_x + mean_y * mean_y + mean_z * mean_z)
    unit_x = mean_x * inverse_norm
    unit_y = mean_y * inverse_norm
    unit_z = mean_z * inverse_norm
    square_x = unit_x * unit_x
    square_y = unit_y * unit_y
    square_z = unit_z * unit_z
    return [
        HARM_ZERO * jnp.ones_like(unit_x),
        -HARM_ONE * unit_y,
        HARM_ONE * unit_z,
        -HARM_ONE * unit_x,
        HARM_TWO[0] * unit_x * unit_y,
        HARM_TWO[1] * unit_y * unit_z,
        HARM_TWO[2] * (2.0 * square_z - square_x - square_y),
        HARM_TWO[3] * unit_x * unit_z,
        HARM_TWO[4] * (square_x - square_y),
        HARM_THREE[0] * unit_y * (3.0 * square_x - square_y),
        HARM_THREE[1] * unit_x * unit_y * unit_z,
        HARM_THREE[2] * unit_y * (4.0 * square_z - square_x - square_y),
        HARM_THREE[3] * unit_z * (2.0 * square_z - 3.0 * square_x - 3.0 * square_y),
        HARM_THREE[4] * unit_x * (4.0 * square_z - square_x - square_y),
        HARM_THREE[5] * unit_z * (square_x - square_y),
        HARM_THREE[6] * unit_x * (square_x - 3.0 * square_y),
    ]


def project(param):
    mean_x, mean_y, mean_z = param(0), param(1), param(2)
    scales = [jnp.exp(param(3 + axis)) for axis in range(3)]
    quat = [param(6 + part) for part in range(4)]
    quat_norm = jnp.sqrt(quat[0] * quat[0] + quat[1] * quat[1] + quat[2] * quat[2] + quat[3] * quat[3])
    quat_w, quat_x, quat_y, quat_z = (part / quat_norm for part in quat)
    rotation = [
        [
            1.0 - 2.0 * (quat_y * quat_y + quat_z * quat_z),
            2.0 * (quat_x * quat_y - quat_w * quat_z),
            2.0 * (quat_x * quat_z + quat_w * quat_y),
        ],
        [
            2.0 * (quat_x * quat_y + quat_w * quat_z),
            1.0 - 2.0 * (quat_x * quat_x + quat_z * quat_z),
            2.0 * (quat_y * quat_z - quat_w * quat_x),
        ],
        [
            2.0 * (quat_x * quat_z - quat_w * quat_y),
            2.0 * (quat_y * quat_z + quat_w * quat_x),
            1.0 - 2.0 * (quat_x * quat_x + quat_y * quat_y),
        ],
    ]
    scaled = [[rotation[row][col] * scales[col] for col in range(3)] for row in range(3)]
    sigma = [
        [sum(scaled[row][inner] * scaled[col][inner] for inner in range(3)) for col in range(3)]
        for row in range(3)
    ]
    inverse_depth = 1.0 / mean_z
    jac_diag = FOCAL_LENGTH * inverse_depth
    jac_first = -FOCAL_LENGTH * mean_x * inverse_depth * inverse_depth
    jac_second = -FOCAL_LENGTH * mean_y * inverse_depth * inverse_depth
    upper_row = [jac_diag * sigma[0][col] + jac_first * sigma[2][col] for col in range(3)]
    lower_row = [jac_diag * sigma[1][col] + jac_second * sigma[2][col] for col in range(3)]
    entry_a = upper_row[0] * jac_diag + upper_row[2] * jac_first + BLUR_TERM
    entry_b = upper_row[1] * jac_diag + upper_row[2] * jac_second
    entry_c = lower_row[1] * jac_diag + lower_row[2] * jac_second + BLUR_TERM
    determinant = entry_a * entry_c - entry_b * entry_b
    centre_u = FOCAL_LENGTH * mean_x * inverse_depth + CENTRE_SHIFT
    centre_v = FOCAL_LENGTH * mean_y * inverse_depth + CENTRE_SHIFT
    log_opacity = jnp.maximum(-jnp.log2(1.0 + jnp.exp(-param(10))), -10000.0)
    basis = sh_basis(mean_x, mean_y, mean_z)
    colour = [0.5 + sum(param(11 + 16 * c + k) * basis[k] for k in range(16)) for c in range(3)]
    attributes = [
        colour[0],
        colour[1],
        centre_u,
        centre_v,
        log_opacity,
        entry_c / determinant,
        -entry_b / determinant,
        entry_a / determinant,
        colour[2],
    ]
    kept = [jnp.where(value == value, jnp.clip(value, -1e30, 1e30), 0.0) for value in attributes]
    return kept, basis


def split_three(values):
    high = values.astype(BF16)
    rest = values - high.astype(F32)
    middle = rest.astype(BF16)
    low = (rest - middle.astype(F32)).astype(BF16)
    return high, middle, low


def split_two(values):
    high = values.astype(BF16)
    return high, (values - high.astype(F32)).astype(BF16)


def one_hot(low_index):
    rows = lax.broadcasted_iota(jnp.int32, (UNIT, UNIT), 0)
    return jnp.where(rows == low_index, 1.0, 0.0).astype(BF16)


def build_table(rows_ref, table_ref, groups):
    nothing = jnp.zeros((1, UNIT), F32)
    for pair in range(groups // 2):
        firsts, seconds = [], []
        for q in (2 * pair, 2 * pair + 1):
            halves = [rows_ref[pl.ds(18 * q + 9 * half, 9), :] for half in range(2)]
            both = jnp.concatenate(halves, axis=1)
            wanted = jnp.concatenate([both[:5], both[8:9]], axis=0)
            first, second, third = (part.astype(F32) for part in split_three(wanted))
            firsts += [first, third[2:4]]
            seconds += [second, third[4:5], nothing]
        for index, pieces in enumerate((firsts, seconds)):
            table_ref[pl.ds(8 * groups * index + 16 * pair, 16), :] = jnp.concatenate(pieces, axis=0).astype(BF16)


def gather_block(entries, table_ref, groups):
    every = jnp.dot(table_ref[...], one_hot(entries & (UNIT - 1)), preferred_element_type=F32)
    high_rows = jnp.broadcast_to(entries >> 8, (8, UNIT))
    picked = [jnp.zeros((8, UNIT), F32)] * 2
    for q in range(groups):
        member = high_rows == q
        for index in range(2):
            start = 8 * groups * index + 8 * q
            picked[index] = jnp.where(member, every[start : start + 8], picked[index])
    thirds = jnp.concatenate(
        [jnp.zeros((2, UNIT), F32), picked[0][6:8], picked[1][6:7], jnp.zeros((3, UNIT), F32)], axis=0
    )
    return (picked[0] + picked[1]) + thirds


def gather_lanes(entries, rows_ref, attributes, count):
    lane = entries & (LANES - 1)
    high = entries >> 7
    picked = [jnp.zeros((8, LANES), F32) for a in attributes]
    for k in range(count):
        member = high == k
        for index, a in enumerate(attributes):
            row = jnp.broadcast_to(rows_ref[pl.ds(ATTRS * k + a, 1), :], (8, LANES))
            found = jnp.take_along_axis(row, lane, axis=1, mode="promise_in_bounds")
            picked[index] = jnp.where(member, found, picked[index])
    return picked


def scatter_terms(entries, values, groups):
    chosen = one_hot(entries & (UNIT - 1))
    group_rows = lax.broadcasted_iota(jnp.int32, (groups, UNIT), 0)
    member = jnp.where(group_rows == (entries >> 8), 1.0, 0.0).astype(BF16)
    high, low = split_two(values)
    rows = [member * part[c : c + 1] for part in (high, low) for c in range(3)]
    return jnp.concatenate(rows, axis=0), chosen


def dot_transposed(left, right):
    return lax.dot_general(left, right, (((1,), (1,)), ((), ())), preferred_element_type=F32)


OWN_UNROLL = 32


def own_kernel(gaussians, index_hbm, send_ref, basis_ref, params, rows_ref, table_ref, index_ref, sems, index_sem):
    def fetch(k):
        return pltpu.make_async_copy(
            gaussians.at[:, pl.ds(pl.multiple_of(k * LANES, LANES), LANES)],
            params.at[pl.ds(pl.multiple_of(k * PAD_PARAMS, PAD_PARAMS), PARAMS), :],
            sems.at[k],
        )

    def start(k, carry):
        fetch(k).start()
        return carry

    lax.fori_loop(0, OWNED // LANES, start, 0)
    index_copy = pltpu.make_async_copy(index_hbm, index_ref, index_sem)
    index_copy.start()

    def group(kb, carry):
        for k in range(8):
            fetch(8 * kb + k).wait()

        def param(a):
            return params[pl.ds(kb * 8 * PAD_PARAMS + a, 8, stride=PAD_PARAMS), :]

        attributes, basis = project(param)
        for a in range(ATTRS):
            rows_ref[pl.ds(kb * 8 * ATTRS + a, 8, stride=ATTRS), :] = attributes[a]
        for k in range(16):
            basis_ref[pl.ds(kb * 8 * 16 + k, 8, stride=16), :] = basis[k]
        return carry

    lax.fori_loop(0, OWNED // LANES // 8, group, 0)
    build_table(rows_ref, table_ref, Q_OWN)
    index_copy.wait()

    def blocks(i, carry):
        index_rows = index_ref[pl.ds(pl.multiple_of(2 * OWN_UNROLL * i, 8), 2 * OWN_UNROLL), :]
        base = pl.multiple_of(i * (18 * OWN_UNROLL), 8)
        for group in range(OWN_UNROLL // 4):
            found = gather_lanes(index_rows[8 * group : 8 * group + 8], rows_ref, FORM, OWNED // LANES)
            for a, values in zip(FORM, found):
                send_ref[pl.ds(base + 8 * ATTRS * group + a, 8, stride=ATTRS), :] = values
        for j in range(OWN_UNROLL):
            entries = jnp.concatenate([index_rows[2 * j : 2 * j + 1], index_rows[2 * j + 1 : 2 * j + 2]], axis=1)
            picked = gather_block(entries, table_ref, Q_OWN)
            for half in range(2):
                row = base + 18 * j + 9 * half
                lanes = slice(LANES * half, LANES * half + LANES)
                send_ref[pl.ds(row, 5), :] = picked[:5, lanes]
                send_ref[pl.ds(row + 8, 1), :] = picked[5:6, lanes]
        return carry

    lax.fori_loop(0, PEERS // 2 // OWN_UNROLL, blocks, 0)


GATHER_UNROLL = 8
RENDER_UNROLL = 8
MOST = TILE_DEV * BLOCKS
LISTED = MOST + 8


def render_kernel(
    received,
    slots_ref,
    cot_ref,
    counts_ref,
    rank_ref,
    image_ref,
    grad_ref,
    table_ref,
    triangle_ref,
    entries_ref,
    attr_ref,
    halves_ref,
    form_ref,
    gone_ref,
    total_ref,
    picture_ref,
    listed,
):
    build_table(received, table_ref, Q_SLOT)
    before = lax.broadcasted_iota(jnp.int32, (UNIT, UNIT), 0)
    after = lax.broadcasted_iota(jnp.int32, (UNIT, UNIT), 1)
    triangle = jnp.where(before < after, 1.0, 0.0).astype(BF16)
    triangle_ref[...] = triangle
    picture_ref[...] = jnp.zeros_like(picture_ref)
    total_ref[...] = jnp.zeros_like(total_ref)

    def list_tile(t, n):
        count = counts_ref[t]

        def list_block(b, n):
            listed[n] = t * 8 + b
            row = slots_ref[t, pl.ds(b, 1), :]
            entries_ref[n] = row
            halves_ref[pl.ds(2 * n, 1), :] = row[:, :LANES]
            halves_ref[pl.ds(2 * n + 1, 1), :] = row[:, LANES:]
            return n + 1

        return lax.fori_loop(0, count, list_block, n)

    live = lax.fori_loop(0, TILE_DEV, list_tile, 0)
    for extra in range(8):
        listed[live + extra] = TILE_DEV * 8
        entries_ref[live + extra] = jnp.zeros((1, UNIT), jnp.int32)
        halves_ref[pl.ds(2 * (live + extra), 2), :] = jnp.zeros((2, LANES), jnp.int32)

    def gather_step(i, carry):
        for group in range(GATHER_UNROLL // 4):
            row = pl.multiple_of(i * (2 * GATHER_UNROLL), 8) + 8 * group
            found = gather_lanes(halves_ref[pl.ds(row, 8), :], received, FORM, PEERS)
            for index in range(3):
                form_ref[index, pl.ds(row, 8), :] = found[index]
        for j in range(GATHER_UNROLL):
            n = i * GATHER_UNROLL + j
            attr_ref[n] = gather_block(entries_ref[n], table_ref, Q_SLOT)
        return carry

    lax.fori_loop(0, (live + GATHER_UNROLL - 1) // GATHER_UNROLL, gather_step, 0)

    rank = rank_ref[0]
    lane_ones = jnp.zeros((5, UNIT), F32)
    across = lax.broadcasted_iota(jnp.int32, (8, UNIT), 0).astype(F32)

    def render_one(n):
        code = listed[n]
        t = code >> 3
        source = jnp.minimum(t, TILE_DEV - 1)
        first = (code & 7) == 0
        local_tile = (rank * TILE_DEV + t) % 256
        origin_x = (16 * (local_tile % 16)).astype(F32) + 0.5
        origin_y = (16 * (local_tile // 16)).astype(F32) + 0.5
        picked = attr_ref[n]

        def wide(row):
            return jnp.broadcast_to(picked[row : row + 1], (8, UNIT))

        centre_u, centre_v = wide(2), wide(3)
        def form(index):
            halves = [form_ref[index, pl.ds(2 * n + half, 1), :] for half in range(2)]
            return jnp.broadcast_to(jnp.concatenate(halves, axis=1), (8, UNIT))

        form_a = form(0) * (-0.5 * LOG2E)
        form_b = form(1) * (-LOG2E)
        form_c = form(2) * (-0.5 * LOG2E)
        log_opacity = wide(4)
        constant, linear = [], []
        for half in range(2):
            delta_x = (across + (origin_x + 8.0 * half)) - centre_u
            constant.append(form_a * delta_x * delta_x + log_opacity)
            linear.append(form_b * delta_x)
        powers = []
        for y in range(16):
            delta_y = (origin_y + y) - centre_v
            bent = form_c * delta_y
            for half in range(2):
                powers.append(constant[half] + delta_y * (linear[half] + bent))
        alpha = jnp.exp2(jnp.concatenate(powers, axis=0))
        log_keep = jnp.log2(1.0 - alpha)
        sums = jnp.dot(jnp.concatenate(split_two(log_keep), axis=0), triangle_ref[...], preferred_element_type=F32)
        cot = jnp.concatenate([cot_ref[c, pl.ds(source, 1), :] for c in range(3)] + [lane_ones], axis=0)
        cot_columns = jnp.transpose(cot)
        kept = jnp.where(first, 0.0, 1.0)
        back = [[jnp.zeros((8, LANES), F32) for half in range(2)] for c in range(3)]
        weights = []
        for p in range(UNIT // 8):
            rows = slice(8 * p, 8 * p + 8)
            gone = gone_ref[pl.ds(8 * p, 8), :] * kept
            earlier = (sums[rows] + sums[UNIT + 8 * p : UNIT + 8 * p + 8]) + jnp.concatenate([gone, gone], axis=1)
            weight = alpha[rows] * jnp.exp2(earlier)
            last = (earlier + log_keep[rows])[:, UNIT - 1 : UNIT]
            gone_ref[pl.ds(8 * p, 8), :] = jnp.broadcast_to(last, (8, LANES))
            for c in range(3):
                column = jnp.broadcast_to(cot_columns[rows, c : c + 1], (8, LANES))
                for half in range(2):
                    back[c][half] += column * weight[:, LANES * half : LANES * half + LANES]
            weights.append(weight)
        weight_high, weight_low = split_two(jnp.concatenate(weights, axis=0))
        columns = jnp.concatenate([picked[0:2], picked[5:6], lane_ones], axis=0)
        colour_high, colour_low = split_two(columns)
        nothing = jnp.zeros((8, UNIT), BF16)
        left = jnp.concatenate(
            [
                jnp.concatenate([colour_high, colour_low], axis=0),
                jnp.concatenate([colour_high, nothing], axis=0),
            ],
            axis=1,
        )
        seen = dot_transposed(left, jnp.concatenate([weight_high, weight_low], axis=1))
        seen = seen[:8] + seen[8:]
        picture_ref[t] = jnp.where(first, seen, picture_ref[t] + seen)
        sums_back = [
            jnp.sum(jnp.concatenate(back[c], axis=1), axis=0, keepdims=True) for c in range(3)
        ]
        return jnp.where(t < TILE_DEV, jnp.concatenate(sums_back, axis=0), 0.0)

    def scatter_pair(n, values):
        lefts, rights = [], []
        for j in range(RENDER_UNROLL):
            left, right = scatter_terms(entries_ref[n + j], values[j], Q_SLOT)
            lefts.append(left)
            rights.append(right)
        total_ref[...] += dot_transposed(jnp.concatenate(lefts, axis=1), jnp.concatenate(rights, axis=1))

    def render_step(i, values):
        n = i * RENDER_UNROLL
        scatter_pair(jnp.maximum(n - RENDER_UNROLL, 0), values)
        return tuple(render_one(n + j) for j in range(RENDER_UNROLL))

    gone_ref[...] = jnp.zeros_like(gone_ref)
    steps = (live + RENDER_UNROLL - 1) // RENDER_UNROLL
    nothing_back = tuple(jnp.zeros((3, UNIT), F32) for j in range(RENDER_UNROLL))
    values = lax.fori_loop(0, steps, render_step, nothing_back)
    scatter_pair((steps - 1) * RENDER_UNROLL, values)
    for c in range(3):
        for half in range(2):
            lanes = pl.ds(half * LANES, LANES)
            grad_ref[pl.ds(3 * half + c, Q_SLOT, stride=6), :] = (
                total_ref[pl.ds(c * Q_SLOT, Q_SLOT), lanes]
                + total_ref[pl.ds((3 + c) * Q_SLOT, Q_SLOT), lanes]
            )
    for t in range(TILE_DEV):
        for c in range(3):
            image_ref[c, pl.ds(t, 1), :] = picture_ref[t, pl.ds(c, 1), :]


FINISH_UNROLL = 32


def finish_kernel(returned, index_ref, basis_ref, out_ref, total_ref):
    total_ref[...] = jnp.zeros_like(total_ref)

    def scatter_step(i, carry):
        rows = returned[pl.ds(pl.multiple_of(i * (6 * FINISH_UNROLL), 8), 6 * FINISH_UNROLL), :]
        index_rows = index_ref[pl.ds(pl.multiple_of(2 * FINISH_UNROLL * i, 8), 2 * FINISH_UNROLL), :]
        lefts, rights = [], []
        for j in range(FINISH_UNROLL):
            entries = jnp.concatenate([index_rows[2 * j : 2 * j + 1], index_rows[2 * j + 1 : 2 * j + 2]], axis=1)
            values = jnp.concatenate([rows[6 * j : 6 * j + 3], rows[6 * j + 3 : 6 * j + 6]], axis=1)
            left, right = scatter_terms(entries, values, Q_OWN)
            lefts.append(left)
            rights.append(right)
        total_ref[...] += dot_transposed(jnp.concatenate(lefts, axis=1), jnp.concatenate(rights, axis=1))
        return carry

    lax.fori_loop(0, PEERS // 2 // FINISH_UNROLL, scatter_step, 0)
    for k in range(OWNED // LANES):
        basis = basis_ref[pl.ds(16 * k, 16), :]
        for c in range(3):
            lanes = pl.ds((k % 2) * LANES, LANES)
            grad = (
                total_ref[pl.ds(c * Q_OWN + k // 2, 1), lanes]
                + total_ref[pl.ds((3 + c) * Q_OWN + k // 2, 1), lanes]
            )
            out_ref[pl.ds(16 * c, 16), pl.ds(k * LANES, LANES)] = basis * grad


def exchange(buffer):
    return lax.all_to_all(buffer, AXES, split_axis=0, concat_axis=0, tiled=True)


def per_device(gaussians, send_index, tile_slots, block_count, cotangent):
    vmem = pl.BlockSpec(memory_space=pltpu.VMEM)
    smem = pl.BlockSpec(memory_space=pltpu.SMEM)
    limits = pltpu.CompilerParams(vmem_limit_bytes=VMEM_BYTES)
    shape = jax.ShapeDtypeStruct
    rank = lax.axis_index(AXES).astype(jnp.int32).reshape(1)
    index = send_index.reshape(PEERS, WIDTH)
    send, basis = pl.pallas_call(
        own_kernel,
        out_shape=(shape((ATTRS * PEERS, WIDTH), F32), shape((16 * OWNED // LANES, LANES), F32)),
        in_specs=[pl.BlockSpec(memory_space=pltpu.HBM), pl.BlockSpec(memory_space=pltpu.HBM)],
        out_specs=(vmem, vmem),
        scratch_shapes=[
            pltpu.VMEM((PAD_PARAMS * OWNED // LANES, LANES), F32),
            pltpu.VMEM((ATTRS * OWNED // LANES, LANES), F32),
            pltpu.VMEM((16 * Q_OWN, UNIT), BF16),
            pltpu.VMEM((PEERS, WIDTH), jnp.int32),
            pltpu.SemaphoreType.DMA((OWNED // LANES,)),
            pltpu.SemaphoreType.DMA(()),
        ],
        compiler_params=pltpu.CompilerParams(vmem_limit_bytes=62 * 2**20),
        name="project_and_pack",
    )(gaussians, index)
    received = exchange(send.reshape(PEERS, ATTRS * WIDTH)).reshape(ATTRS * PEERS, WIDTH)
    image, slot_grad = pl.pallas_call(
        render_kernel,
        out_shape=(shape((3, TILE_DEV, UNIT), F32), shape((3 * PEERS, WIDTH), F32)),
        in_specs=[vmem, vmem, vmem, smem, smem],
        out_specs=(vmem, vmem),
        scratch_shapes=[
            pltpu.VMEM((16 * Q_SLOT, UNIT), BF16),
            pltpu.VMEM((UNIT, UNIT), BF16),
            pltpu.VMEM((LISTED, 1, UNIT), jnp.int32),
            pltpu.VMEM((LISTED, 8, UNIT), F32),
            pltpu.VMEM((2 * LISTED, LANES), jnp.int32),
            pltpu.VMEM((3, 2 * LISTED, LANES), F32),
            pltpu.VMEM((UNIT, LANES), F32),
            pltpu.VMEM((6 * Q_SLOT, UNIT), F32),
            pltpu.VMEM((TILE_DEV + 1, 8, UNIT), F32),
            pltpu.SMEM((LISTED,), jnp.int32),
        ],
        compiler_params=limits,
        name="render",
    )(received, tile_slots, cotangent, block_count, rank)
    returned = exchange(slot_grad.reshape(PEERS, 3 * WIDTH)).reshape(3 * PEERS, WIDTH)
    sh_grad = pl.pallas_call(
        finish_kernel,
        out_shape=shape((48, OWNED), F32),
        in_specs=[vmem, vmem, vmem],
        out_specs=vmem,
        scratch_shapes=[pltpu.VMEM((6 * Q_OWN, UNIT), F32)],
        compiler_params=limits,
        name="finish",
    )(returned, index, basis)
    return image, sh_grad


def solution(mesh):
    placed = (
        P(None, AXES),
        P(AXES, None, None),
        P(AXES, None, None),
        P(AXES),
        P(None, AXES, None),
    )
    return jax.shard_map(
        per_device,
        mesh=mesh,
        in_specs=placed,
        out_specs=(P(None, AXES, None), P(None, AXES)),
        check_vma=False,
    )
```

```python
import jax
import jax.numpy as jnp
from jax import lax
from jax.experimental import pallas as pl
from jax.experimental.pallas import tpu as pltpu
from jax.sharding import PartitionSpec as P

AXES = ("cell", "tile")
PEERS = 128
WIDTH = 128
OWNED = 8192
SLOTS = 16384
TILE_DEV = 32
BLOCKS = 4
PARAMS = 59
ATTRS = 9
UNIT = 256
FORM = (5, 6, 7)
Q_OWN = OWNED // UNIT
Q_SLOT = SLOTS // UNIT
LANES = 128
PAD_PARAMS = 64
F32 = jnp.float32
BF16 = jnp.bfloat16
VMEM_BYTES = 48 * 2**20

FOCAL_LENGTH = 256.0
CENTRE_SHIFT = 128.0
BLUR_TERM = 0.3
LOG2E = 1.4426950408889634
HARM_ZERO = 0.28209479177387814
HARM_ONE = 0.4886025119029199
HARM_TWO = (
    1.0925484305920792,
    -1.0925484305920792,
    0.31539156525252005,
    -1.0925484305920792,
    0.5462742152960396,
)
HARM_THREE = (
    -0.5900435899266435,
    2.890611442640554,
    -0.4570457994644658,
    0.3731763325901154,
    -0.4570457994644658,
    1.445305721320277,
    -0.5900435899266435,
)


def sh_basis(mean_x, mean_y, mean_z):
    inverse_norm = 1.0 / jnp.sqrt(mean_x * mean_x + mean_y * mean_y + mean_z * mean_z)
    unit_x = mean_x * inverse_norm
    unit_y = mean_y * inverse_norm
    unit_z = mean_z * inverse_norm
    square_x = unit_x * unit_x
    square_y = unit_y * unit_y
    square_z = unit_z * unit_z
    return [
        HARM_ZERO * jnp.ones_like(unit_x),
        -HARM_ONE * unit_y,
        HARM_ONE * unit_z,
        -HARM_ONE * unit_x,
        HARM_TWO[0] * unit_x * unit_y,
        HARM_TWO[1] * unit_y * unit_z,
        HARM_TWO[2] * (2.0 * square_z - square_x - square_y),
        HARM_TWO[3] * unit_x * unit_z,
        HARM_TWO[4] * (square_x - square_y),
        HARM_THREE[0] * unit_y * (3.0 * square_x - square_y),
        HARM_THREE[1] * unit_x * unit_y * unit_z,
        HARM_THREE[2] * unit_y * (4.0 * square_z - square_x - square_y),
        HARM_THREE[3] * unit_z * (2.0 * square_z - 3.0 * square_x - 3.0 * square_y),
        HARM_THREE[4] * unit_x * (4.0 * square_z - square_x - square_y),
        HARM_THREE[5] * unit_z * (square_x - square_y),
        HARM_THREE[6] * unit_x * (square_x - 3.0 * square_y),
    ]


def project(param):
    mean_x, mean_y, mean_z = param(0), param(1), param(2)
    scales = [jnp.exp(param(3 + axis)) for axis in range(3)]
    quat = [param(6 + part) for part in range(4)]
    quat_norm = jnp.sqrt(quat[0] * quat[0] + quat[1] * quat[1] + quat[2] * quat[2] + quat[3] * quat[3])
    quat_w, quat_x, quat_y, quat_z = (part / quat_norm for part in quat)
    rotation = [
        [
            1.0 - 2.0 * (quat_y * quat_y + quat_z * quat_z),
            2.0 * (quat_x * quat_y - quat_w * quat_z),
            2.0 * (quat_x * quat_z + quat_w * quat_y),
        ],
        [
            2.0 * (quat_x * quat_y + quat_w * quat_z),
            1.0 - 2.0 * (quat_x * quat_x + quat_z * quat_z),
            2.0 * (quat_y * quat_z - quat_w * quat_x),
        ],
        [
            2.0 * (quat_x * quat_z - quat_w * quat_y),
            2.0 * (quat_y * quat_z + quat_w * quat_x),
            1.0 - 2.0 * (quat_x * quat_x + quat_y * quat_y),
        ],
    ]
    scaled = [[rotation[row][col] * scales[col] for col in range(3)] for row in range(3)]
    sigma = [
        [sum(scaled[row][inner] * scaled[col][inner] for inner in range(3)) for col in range(3)]
        for row in range(3)
    ]
    inverse_depth = 1.0 / mean_z
    jac_diag = FOCAL_LENGTH * inverse_depth
    jac_first = -FOCAL_LENGTH * mean_x * inverse_depth * inverse_depth
    jac_second = -FOCAL_LENGTH * mean_y * inverse_depth * inverse_depth
    upper_row = [jac_diag * sigma[0][col] + jac_first * sigma[2][col] for col in range(3)]
    lower_row = [jac_diag * sigma[1][col] + jac_second * sigma[2][col] for col in range(3)]
    entry_a = upper_row[0] * jac_diag + upper_row[2] * jac_first + BLUR_TERM
    entry_b = upper_row[1] * jac_diag + upper_row[2] * jac_second
    entry_c = lower_row[1] * jac_diag + lower_row[2] * jac_second + BLUR_TERM
    determinant = entry_a * entry_c - entry_b * entry_b
    centre_u = FOCAL_LENGTH * mean_x * inverse_depth + CENTRE_SHIFT
    centre_v = FOCAL_LENGTH * mean_y * inverse_depth + CENTRE_SHIFT
    log_opacity = jnp.maximum(-jnp.log2(1.0 + jnp.exp(-param(10))), -10000.0)
    basis = sh_basis(mean_x, mean_y, mean_z)
    colour = [0.5 + sum(param(11 + 16 * c + k) * basis[k] for k in range(16)) for c in range(3)]
    attributes = [
        colour[0],
        colour[1],
        centre_u,
        centre_v,
        log_opacity,
        entry_c / determinant,
        -entry_b / determinant,
        entry_a / determinant,
        colour[2],
    ]
    kept = [jnp.where(value == value, jnp.clip(value, -1e30, 1e30), 0.0) for value in attributes]
    return kept, basis


def split_three(values):
    high = values.astype(BF16)
    rest = values - high.astype(F32)
    middle = rest.astype(BF16)
    low = (rest - middle.astype(F32)).astype(BF16)
    return high, middle, low


def split_two(values):
    high = values.astype(BF16)
    return high, (values - high.astype(F32)).astype(BF16)


def one_hot(low_index):
    rows = lax.broadcasted_iota(jnp.int32, (UNIT, UNIT), 0)
    return jnp.where(rows == low_index, 1.0, 0.0).astype(BF16)


def build_table(rows_ref, table_ref, groups):
    nothing = jnp.zeros((1, UNIT), F32)
    for pair in range(groups // 2):
        firsts, seconds = [], []
        for q in (2 * pair, 2 * pair + 1):
            halves = [rows_ref[pl.ds(18 * q + 9 * half, 9), :] for half in range(2)]
            both = jnp.concatenate(halves, axis=1)
            wanted = jnp.concatenate([both[:5], both[8:9]], axis=0)
            first, second, third = (part.astype(F32) for part in split_three(wanted))
            firsts += [first, third[2:4]]
            seconds += [second, third[4:5], nothing]
        for index, pieces in enumerate((firsts, seconds)):
            table_ref[pl.ds(8 * groups * index + 16 * pair, 16), :] = jnp.concatenate(pieces, axis=0).astype(BF16)


def gather_block(entries, table_ref, groups):
    every = jnp.dot(table_ref[...], one_hot(entries & (UNIT - 1)), preferred_element_type=F32)
    high_rows = jnp.broadcast_to(entries >> 8, (8, UNIT))
    picked = [jnp.zeros((8, UNIT), F32)] * 2
    for q in range(groups):
        member = high_rows == q
        for index in range(2):
            start = 8 * groups * index + 8 * q
            picked[index] = jnp.where(member, every[start : start + 8], picked[index])
    thirds = jnp.concatenate(
        [jnp.zeros((2, UNIT), F32), picked[0][6:8], picked[1][6:7], jnp.zeros((3, UNIT), F32)], axis=0
    )
    return (picked[0] + picked[1]) + thirds


def gather_lanes(entries, rows_ref, attributes, count):
    lane = entries & (LANES - 1)
    high = entries >> 7
    picked = [jnp.zeros((8, LANES), F32) for a in attributes]
    for k in range(count):
        member = high == k
        for index, a in enumerate(attributes):
            row = jnp.broadcast_to(rows_ref[pl.ds(ATTRS * k + a, 1), :], (8, LANES))
            found = jnp.take_along_axis(row, lane, axis=1, mode="promise_in_bounds")
            picked[index] = jnp.where(member, found, picked[index])
    return picked


def scatter_terms(entries, values, groups):
    chosen = one_hot(entries & (UNIT - 1))
    group_rows = lax.broadcasted_iota(jnp.int32, (groups, UNIT), 0)
    member = jnp.where(group_rows == (entries >> 8), 1.0, 0.0).astype(BF16)
    high, low = split_two(values)
    rows = [member * part[c : c + 1] for part in (high, low) for c in range(3)]
    return jnp.concatenate(rows, axis=0), chosen


def dot_transposed(left, right):
    return lax.dot_general(left, right, (((1,), (1,)), ((), ())), preferred_element_type=F32)


OWN_UNROLL = 32


def own_kernel(gaussians, index_hbm, send_ref, basis_ref, params, rows_ref, table_ref, index_ref, sems, index_sem):
    def fetch(k):
        return pltpu.make_async_copy(
            gaussians.at[:, pl.ds(pl.multiple_of(k * LANES, LANES), LANES)],
            params.at[pl.ds(pl.multiple_of(k * PAD_PARAMS, PAD_PARAMS), PARAMS), :],
            sems.at[k],
        )

    def start(k, carry):
        fetch(k).start()
        return carry

    lax.fori_loop(0, OWNED // LANES, start, 0)
    index_copy = pltpu.make_async_copy(index_hbm, index_ref, index_sem)
    index_copy.start()

    def group(kb, carry):
        for k in range(8):
            fetch(8 * kb + k).wait()

        def param(a):
            return params[pl.ds(kb * 8 * PAD_PARAMS + a, 8, stride=PAD_PARAMS), :]

        attributes, basis = project(param)
        for a in range(ATTRS):
            rows_ref[pl.ds(kb * 8 * ATTRS + a, 8, stride=ATTRS), :] = attributes[a]
        for k in range(16):
            basis_ref[pl.ds(kb * 8 * 16 + k, 8, stride=16), :] = basis[k]
        return carry

    lax.fori_loop(0, OWNED // LANES // 8, group, 0)
    build_table(rows_ref, table_ref, Q_OWN)
    index_copy.wait()

    def blocks(i, carry):
        index_rows = index_ref[pl.ds(pl.multiple_of(2 * OWN_UNROLL * i, 8), 2 * OWN_UNROLL), :]
        base = pl.multiple_of(i * (18 * OWN_UNROLL), 8)
        for group in range(OWN_UNROLL // 4):
            found = gather_lanes(index_rows[8 * group : 8 * group + 8], rows_ref, FORM, OWNED // LANES)
            for a, values in zip(FORM, found):
                send_ref[pl.ds(base + 8 * ATTRS * group + a, 8, stride=ATTRS), :] = values
        for j in range(OWN_UNROLL):
            entries = jnp.concatenate([index_rows[2 * j : 2 * j + 1], index_rows[2 * j + 1 : 2 * j + 2]], axis=1)
            picked = gather_block(entries, table_ref, Q_OWN)
            for half in range(2):
                row = base + 18 * j + 9 * half
                lanes = slice(LANES * half, LANES * half + LANES)
                send_ref[pl.ds(row, 5), :] = picked[:5, lanes]
                send_ref[pl.ds(row + 8, 1), :] = picked[5:6, lanes]
        return carry

    lax.fori_loop(0, PEERS // 2 // OWN_UNROLL, blocks, 0)


GATHER_UNROLL = 8
RENDER_UNROLL = 8
MOST = TILE_DEV * BLOCKS
LISTED = MOST + 8


def render_kernel(
    received,
    slots_ref,
    cot_ref,
    counts_ref,
    rank_ref,
    image_ref,
    grad_ref,
    table_ref,
    triangle_ref,
    entries_ref,
    attr_ref,
    halves_ref,
    form_ref,
    gone_ref,
    total_ref,
    picture_ref,
    listed,
):
    build_table(received, table_ref, Q_SLOT)
    before = lax.broadcasted_iota(jnp.int32, (UNIT, UNIT), 0)
    after = lax.broadcasted_iota(jnp.int32, (UNIT, UNIT), 1)
    triangle = jnp.where(before < after, 1.0, 0.0).astype(BF16)
    triangle_ref[...] = triangle
    picture_ref[...] = jnp.zeros_like(picture_ref)
    total_ref[...] = jnp.zeros_like(total_ref)

    live = jnp.int32(0)
    for t in range(TILE_DEV):
        for b in range(BLOCKS):
            listed[live + b] = t * 8 + b
            row = slots_ref[t, pl.ds(b, 1), :]
            entries_ref[live + b] = row
            for half in range(2):
                halves_ref[pl.ds(2 * (live + b) + half, 1), :] = row[:, LANES * half : LANES * half + LANES]
        live = live + counts_ref[t]
    for extra in range(8):
        listed[live + extra] = TILE_DEV * 8
        entries_ref[live + extra] = jnp.zeros((1, UNIT), jnp.int32)
        halves_ref[pl.ds(2 * (live + extra), 2), :] = jnp.zeros((2, LANES), jnp.int32)

    def gather_step(i, carry):
        for group in range(GATHER_UNROLL // 4):
            row = pl.multiple_of(i * (2 * GATHER_UNROLL), 8) + 8 * group
            found = gather_lanes(halves_ref[pl.ds(row, 8), :], received, FORM, PEERS)
            for index in range(3):
                form_ref[index, pl.ds(row, 8), :] = found[index]
        for j in range(GATHER_UNROLL):
            n = i * GATHER_UNROLL + j
            attr_ref[n] = gather_block(entries_ref[n], table_ref, Q_SLOT)
        return carry

    lax.fori_loop(0, (live + GATHER_UNROLL - 1) // GATHER_UNROLL, gather_step, 0)

    rank = rank_ref[0]
    lane_ones = jnp.zeros((5, UNIT), F32)
    across = lax.broadcasted_iota(jnp.int32, (8, UNIT), 0).astype(F32)

    def render_one(n):
        code = listed[n]
        t = code >> 3
        source = jnp.minimum(t, TILE_DEV - 1)
        first = (code & 7) == 0
        local_tile = (rank * TILE_DEV + t) % 256
        origin_x = (16 * (local_tile % 16)).astype(F32) + 0.5
        origin_y = (16 * (local_tile // 16)).astype(F32) + 0.5
        picked = attr_ref[n]

        def wide(row):
            return jnp.broadcast_to(picked[row : row + 1], (8, UNIT))

        centre_u, centre_v = wide(2), wide(3)
        def form(index):
            halves = [form_ref[index, pl.ds(2 * n + half, 1), :] for half in range(2)]
            return jnp.broadcast_to(jnp.concatenate(halves, axis=1), (8, UNIT))

        form_a = form(0) * (-0.5 * LOG2E)
        form_b = form(1) * (-LOG2E)
        form_c = form(2) * (-0.5 * LOG2E)
        log_opacity = wide(4)
        constant, linear = [], []
        for half in range(2):
            delta_x = (across + (origin_x + 8.0 * half)) - centre_u
            constant.append(form_a * delta_x * delta_x + log_opacity)
            linear.append(form_b * delta_x)
        powers = []
        for y in range(16):
            delta_y = (origin_y + y) - centre_v
            bent = form_c * delta_y
            for half in range(2):
                powers.append(constant[half] + delta_y * (linear[half] + bent))
        alpha = jnp.exp2(jnp.concatenate(powers, axis=0))
        log_keep = jnp.log2(1.0 - alpha)
        sums = jnp.dot(jnp.concatenate(split_two(log_keep), axis=0), triangle_ref[...], preferred_element_type=F32)
        cot = jnp.concatenate([cot_ref[c, pl.ds(source, 1), :] for c in range(3)] + [lane_ones], axis=0)
        cot_columns = [jnp.transpose(jnp.broadcast_to(cot[c : c + 1], (LANES, UNIT))) for c in range(3)]
        kept = jnp.where(first, 0.0, 1.0)
        back = [[jnp.zeros((8, LANES), F32) for half in range(2)] for c in range(3)]
        weights = []
        for p in range(UNIT // 8):
            rows = slice(8 * p, 8 * p + 8)
            gone = gone_ref[pl.ds(8 * p, 8), :] * kept
            earlier = (sums[rows] + sums[UNIT + 8 * p : UNIT + 8 * p + 8]) + jnp.concatenate([gone, gone], axis=1)
            weight = alpha[rows] * jnp.exp2(earlier)
            last = (earlier + log_keep[rows])[:, UNIT - 1 : UNIT]
            gone_ref[pl.ds(8 * p, 8), :] = jnp.broadcast_to(last, (8, LANES))
            weights.append(weight)
        for c in range(3):
            for p in range(UNIT // 8):
                column = cot_columns[c][8 * p : 8 * p + 8]
                for half in range(2):
                    back[c][half] += column * weights[p][:, LANES * half : LANES * half + LANES]
        weight_high, weight_low = split_two(jnp.concatenate(weights, axis=0))
        columns = jnp.concatenate([picked[0:2], picked[5:6], lane_ones], axis=0)
        colour_high, colour_low = split_two(columns)
        nothing = jnp.zeros((8, UNIT), BF16)
        left = jnp.concatenate(
            [
                jnp.concatenate([colour_high, colour_low], axis=0),
                jnp.concatenate([colour_high, nothing], axis=0),
            ],
            axis=1,
        )
        seen = dot_transposed(left, jnp.concatenate([weight_high, weight_low], axis=1))
        seen = seen[:8] + seen[8:]
        picture_ref[t] = jnp.where(first, seen, picture_ref[t] + seen)
        sums_back = [
            jnp.sum(jnp.concatenate(back[c], axis=1), axis=0, keepdims=True) for c in range(3)
        ]
        return jnp.where(t < TILE_DEV, jnp.concatenate(sums_back, axis=0), 0.0)

    def scatter_pair(n, values):
        lefts, rights = [], []
        for j in range(RENDER_UNROLL):
            left, right = scatter_terms(entries_ref[n + j], values[j], Q_SLOT)
            lefts.append(left)
            rights.append(right)
        total_ref[...] += dot_transposed(jnp.concatenate(lefts, axis=1), jnp.concatenate(rights, axis=1))

    def render_step(i, values):
        n = i * RENDER_UNROLL
        scatter_pair(jnp.maximum(n - RENDER_UNROLL, 0), values)
        return tuple(render_one(n + j) for j in range(RENDER_UNROLL))

    gone_ref[...] = jnp.zeros_like(gone_ref)
    steps = (live + RENDER_UNROLL - 1) // RENDER_UNROLL
    nothing_back = tuple(jnp.zeros((3, UNIT), F32) for j in range(RENDER_UNROLL))
    values = lax.fori_loop(0, steps, render_step, nothing_back)
    scatter_pair((steps - 1) * RENDER_UNROLL, values)
    for c in range(3):
        for half in range(2):
            lanes = pl.ds(half * LANES, LANES)
            grad_ref[pl.ds(3 * half + c, Q_SLOT, stride=6), :] = (
                total_ref[pl.ds(c * Q_SLOT, Q_SLOT), lanes]
                + total_ref[pl.ds((3 + c) * Q_SLOT, Q_SLOT), lanes]
            )
    for t in range(TILE_DEV):
        for c in range(3):
            image_ref[c, pl.ds(t, 1), :] = picture_ref[t, pl.ds(c, 1), :]


FINISH_UNROLL = 32


def finish_kernel(returned, index_ref, basis_ref, out_ref, total_ref):
    total_ref[...] = jnp.zeros_like(total_ref)

    def scatter_step(i, carry):
        rows = returned[pl.ds(pl.multiple_of(i * (6 * FINISH_UNROLL), 8), 6 * FINISH_UNROLL), :]
        index_rows = index_ref[pl.ds(pl.multiple_of(2 * FINISH_UNROLL * i, 8), 2 * FINISH_UNROLL), :]
        lefts, rights = [], []
        for j in range(FINISH_UNROLL):
            entries = jnp.concatenate([index_rows[2 * j : 2 * j + 1], index_rows[2 * j + 1 : 2 * j + 2]], axis=1)
            values = jnp.concatenate([rows[6 * j : 6 * j + 3], rows[6 * j + 3 : 6 * j + 6]], axis=1)
            left, right = scatter_terms(entries, values, Q_OWN)
            lefts.append(left)
            rights.append(right)
        total_ref[...] += dot_transposed(jnp.concatenate(lefts, axis=1), jnp.concatenate(rights, axis=1))
        return carry

    lax.fori_loop(0, PEERS // 2 // FINISH_UNROLL, scatter_step, 0)
    for k in range(OWNED // LANES):
        basis = basis_ref[pl.ds(16 * k, 16), :]
        for c in range(3):
            lanes = pl.ds((k % 2) * LANES, LANES)
            grad = (
                total_ref[pl.ds(c * Q_OWN + k // 2, 1), lanes]
                + total_ref[pl.ds((3 + c) * Q_OWN + k // 2, 1), lanes]
            )
            out_ref[pl.ds(16 * c, 16), pl.ds(k * LANES, LANES)] = basis * grad


def exchange(buffer):
    return lax.all_to_all(buffer, AXES, split_axis=0, concat_axis=0, tiled=True)


def per_device(gaussians, send_index, tile_slots, block_count, cotangent):
    vmem = pl.BlockSpec(memory_space=pltpu.VMEM)
    smem = pl.BlockSpec(memory_space=pltpu.SMEM)
    limits = pltpu.CompilerParams(vmem_limit_bytes=VMEM_BYTES)
    shape = jax.ShapeDtypeStruct
    rank = lax.axis_index(AXES).astype(jnp.int32).reshape(1)
    index = send_index.reshape(PEERS, WIDTH)
    send, basis = pl.pallas_call(
        own_kernel,
        out_shape=(shape((ATTRS * PEERS, WIDTH), F32), shape((16 * OWNED // LANES, LANES), F32)),
        in_specs=[pl.BlockSpec(memory_space=pltpu.HBM), pl.BlockSpec(memory_space=pltpu.HBM)],
        out_specs=(vmem, vmem),
        scratch_shapes=[
            pltpu.VMEM((PAD_PARAMS * OWNED // LANES, LANES), F32),
            pltpu.VMEM((ATTRS * OWNED // LANES, LANES), F32),
            pltpu.VMEM((16 * Q_OWN, UNIT), BF16),
            pltpu.VMEM((PEERS, WIDTH), jnp.int32),
            pltpu.SemaphoreType.DMA((OWNED // LANES,)),
            pltpu.SemaphoreType.DMA(()),
        ],
        compiler_params=pltpu.CompilerParams(vmem_limit_bytes=62 * 2**20),
        name="project_and_pack",
    )(gaussians, index)
    received = exchange(send.reshape(PEERS, ATTRS * WIDTH)).reshape(ATTRS * PEERS, WIDTH)
    image, slot_grad = pl.pallas_call(
        render_kernel,
        out_shape=(shape((3, TILE_DEV, UNIT), F32), shape((3 * PEERS, WIDTH), F32)),
        in_specs=[vmem, vmem, vmem, smem, smem],
        out_specs=(vmem, vmem),
        scratch_shapes=[
            pltpu.VMEM((16 * Q_SLOT, UNIT), BF16),
            pltpu.VMEM((UNIT, UNIT), BF16),
            pltpu.VMEM((LISTED, 1, UNIT), jnp.int32),
            pltpu.VMEM((LISTED, 8, UNIT), F32),
            pltpu.VMEM((2 * LISTED, LANES), jnp.int32),
            pltpu.VMEM((3, 2 * LISTED, LANES), F32),
            pltpu.VMEM((UNIT, LANES), F32),
            pltpu.VMEM((6 * Q_SLOT, UNIT), F32),
            pltpu.VMEM((TILE_DEV + 1, 8, UNIT), F32),
            pltpu.SMEM((LISTED,), jnp.int32),
        ],
        compiler_params=limits,
        name="render",
    )(received, tile_slots, cotangent, block_count, rank)
    returned = exchange(slot_grad.reshape(PEERS, 3 * WIDTH)).reshape(3 * PEERS, WIDTH)
    sh_grad = pl.pallas_call(
        finish_kernel,
        out_shape=shape((48, OWNED), F32),
        in_specs=[vmem, vmem, vmem],
        out_specs=vmem,
        scratch_shapes=[pltpu.VMEM((6 * Q_OWN, UNIT), F32)],
        compiler_params=limits,
        name="finish",
    )(returned, index, basis)
    return image, sh_grad


def solution(mesh):
    placed = (
        P(None, AXES),
        P(AXES, None, None),
        P(AXES, None, None),
        P(AXES),
        P(None, AXES, None),
    )
    return jax.shard_map(
        per_device,
        mesh=mesh,
        in_specs=placed,
        out_specs=(P(None, AXES, None), P(None, AXES)),
        check_vma=False,
    )
```

```python
import jax
import jax.numpy as jnp
from jax import lax
from jax.experimental import pallas as pl
from jax.experimental.pallas import tpu as pltpu
from jax.sharding import PartitionSpec as P

AXES = ("cell", "tile")
PEERS = 128
WIDTH = 128
OWNED = 8192
SLOTS = 16384
TILE_DEV = 32
BLOCKS = 4
PARAMS = 59
ATTRS = 9
UNIT = 256
FORM = (5, 6, 7)
Q_OWN = OWNED // UNIT
Q_SLOT = SLOTS // UNIT
LANES = 128
PAD_PARAMS = 64
F32 = jnp.float32
BF16 = jnp.bfloat16
VMEM_BYTES = 48 * 2**20

FOCAL_LENGTH = 256.0
CENTRE_SHIFT = 128.0
BLUR_TERM = 0.3
LOG2E = 1.4426950408889634
HARM_ZERO = 0.28209479177387814
HARM_ONE = 0.4886025119029199
HARM_TWO = (
    1.0925484305920792,
    -1.0925484305920792,
    0.31539156525252005,
    -1.0925484305920792,
    0.5462742152960396,
)
HARM_THREE = (
    -0.5900435899266435,
    2.890611442640554,
    -0.4570457994644658,
    0.3731763325901154,
    -0.4570457994644658,
    1.445305721320277,
    -0.5900435899266435,
)


def sh_basis(mean_x, mean_y, mean_z):
    inverse_norm = 1.0 / jnp.sqrt(mean_x * mean_x + mean_y * mean_y + mean_z * mean_z)
    unit_x = mean_x * inverse_norm
    unit_y = mean_y * inverse_norm
    unit_z = mean_z * inverse_norm
    square_x = unit_x * unit_x
    square_y = unit_y * unit_y
    square_z = unit_z * unit_z
    return [
        HARM_ZERO * jnp.ones_like(unit_x),
        -HARM_ONE * unit_y,
        HARM_ONE * unit_z,
        -HARM_ONE * unit_x,
        HARM_TWO[0] * unit_x * unit_y,
        HARM_TWO[1] * unit_y * unit_z,
        HARM_TWO[2] * (2.0 * square_z - square_x - square_y),
        HARM_TWO[3] * unit_x * unit_z,
        HARM_TWO[4] * (square_x - square_y),
        HARM_THREE[0] * unit_y * (3.0 * square_x - square_y),
        HARM_THREE[1] * unit_x * unit_y * unit_z,
        HARM_THREE[2] * unit_y * (4.0 * square_z - square_x - square_y),
        HARM_THREE[3] * unit_z * (2.0 * square_z - 3.0 * square_x - 3.0 * square_y),
        HARM_THREE[4] * unit_x * (4.0 * square_z - square_x - square_y),
        HARM_THREE[5] * unit_z * (square_x - square_y),
        HARM_THREE[6] * unit_x * (square_x - 3.0 * square_y),
    ]


def project(param):
    mean_x, mean_y, mean_z = param(0), param(1), param(2)
    scales = [jnp.exp(param(3 + axis)) for axis in range(3)]
    quat = [param(6 + part) for part in range(4)]
    quat_norm = jnp.sqrt(quat[0] * quat[0] + quat[1] * quat[1] + quat[2] * quat[2] + quat[3] * quat[3])
    quat_w, quat_x, quat_y, quat_z = (part / quat_norm for part in quat)
    rotation = [
        [
            1.0 - 2.0 * (quat_y * quat_y + quat_z * quat_z),
            2.0 * (quat_x * quat_y - quat_w * quat_z),
            2.0 * (quat_x * quat_z + quat_w * quat_y),
        ],
        [
            2.0 * (quat_x * quat_y + quat_w * quat_z),
            1.0 - 2.0 * (quat_x * quat_x + quat_z * quat_z),
            2.0 * (quat_y * quat_z - quat_w * quat_x),
        ],
        [
            2.0 * (quat_x * quat_z - quat_w * quat_y),
            2.0 * (quat_y * quat_z + quat_w * quat_x),
            1.0 - 2.0 * (quat_x * quat_x + quat_y * quat_y),
        ],
    ]
    scaled = [[rotation[row][col] * scales[col] for col in range(3)] for row in range(3)]
    sigma = [
        [sum(scaled[row][inner] * scaled[col][inner] for inner in range(3)) for col in range(3)]
        for row in range(3)
    ]
    inverse_depth = 1.0 / mean_z
    jac_diag = FOCAL_LENGTH * inverse_depth
    jac_first = -FOCAL_LENGTH * mean_x * inverse_depth * inverse_depth
    jac_second = -FOCAL_LENGTH * mean_y * inverse_depth * inverse_depth
    upper_row = [jac_diag * sigma[0][col] + jac_first * sigma[2][col] for col in range(3)]
    lower_row = [jac_diag * sigma[1][col] + jac_second * sigma[2][col] for col in range(3)]
    entry_a = upper_row[0] * jac_diag + upper_row[2] * jac_first + BLUR_TERM
    entry_b = upper_row[1] * jac_diag + upper_row[2] * jac_second
    entry_c = lower_row[1] * jac_diag + lower_row[2] * jac_second + BLUR_TERM
    determinant = entry_a * entry_c - entry_b * entry_b
    centre_u = FOCAL_LENGTH * mean_x * inverse_depth + CENTRE_SHIFT
    centre_v = FOCAL_LENGTH * mean_y * inverse_depth + CENTRE_SHIFT
    log_opacity = jnp.maximum(-jnp.log2(1.0 + jnp.exp(-param(10))), -10000.0)
    basis = sh_basis(mean_x, mean_y, mean_z)
    colour = [0.5 + sum(param(11 + 16 * c + k) * basis[k] for k in range(16)) for c in range(3)]
    attributes = [
        colour[0],
        colour[1],
        centre_u,
        centre_v,
        log_opacity,
        entry_c / determinant,
        -entry_b / determinant,
        entry_a / determinant,
        colour[2],
    ]
    kept = [jnp.where(value == value, jnp.clip(value, -1e30, 1e30), 0.0) for value in attributes]
    return kept, basis


def split_three(values):
    high = values.astype(BF16)
    rest = values - high.astype(F32)
    middle = rest.astype(BF16)
    low = (rest - middle.astype(F32)).astype(BF16)
    return high, middle, low


def split_two(values):
    high = values.astype(BF16)
    return high, (values - high.astype(F32)).astype(BF16)


def one_hot(low_index):
    rows = lax.broadcasted_iota(jnp.int32, (UNIT, UNIT), 0)
    return jnp.where(rows == low_index, 1.0, 0.0).astype(BF16)


def build_table(rows_ref, table_ref, groups):
    nothing = jnp.zeros((1, UNIT), F32)
    for pair in range(groups // 2):
        firsts, seconds = [], []
        for q in (2 * pair, 2 * pair + 1):
            halves = [rows_ref[pl.ds(18 * q + 9 * half, 9), :] for half in range(2)]
            both = jnp.concatenate(halves, axis=1)
            wanted = jnp.concatenate([both[:5], both[8:9]], axis=0)
            first, second, third = (part.astype(F32) for part in split_three(wanted))
            firsts += [first, third[2:4]]
            seconds += [second, third[4:5], nothing]
        for index, pieces in enumerate((firsts, seconds)):
            table_ref[pl.ds(8 * groups * index + 16 * pair, 16), :] = jnp.concatenate(pieces, axis=0).astype(BF16)


def gather_block(entries, table_ref, groups):
    every = jnp.dot(table_ref[...], one_hot(entries & (UNIT - 1)), preferred_element_type=F32)
    high_rows = jnp.broadcast_to(entries >> 8, (8, UNIT))
    picked = [jnp.zeros((8, UNIT), F32)] * 2
    for q in range(groups):
        member = high_rows == q
        for index in range(2):
            start = 8 * groups * index + 8 * q
            picked[index] = jnp.where(member, every[start : start + 8], picked[index])
    thirds = jnp.concatenate(
        [jnp.zeros((2, UNIT), F32), picked[0][6:8], picked[1][6:7], jnp.zeros((3, UNIT), F32)], axis=0
    )
    return (picked[0] + picked[1]) + thirds


def gather_lanes(entries, rows_ref, attributes, count):
    lane = entries & (LANES - 1)
    high = entries >> 7
    picked = [jnp.zeros((8, LANES), F32) for a in attributes]
    for k in range(count):
        member = high == k
        for index, a in enumerate(attributes):
            row = jnp.broadcast_to(rows_ref[pl.ds(ATTRS * k + a, 1), :], (8, LANES))
            found = jnp.take_along_axis(row, lane, axis=1, mode="promise_in_bounds")
            picked[index] = jnp.where(member, found, picked[index])
    return picked


def scatter_terms(entries, values, groups):
    chosen = one_hot(entries & (UNIT - 1))
    group_rows = lax.broadcasted_iota(jnp.int32, (groups, UNIT), 0)
    member = jnp.where(group_rows == (entries >> 8), 1.0, 0.0).astype(BF16)
    high, low = split_two(values)
    rows = [member * part[c : c + 1] for part in (high, low) for c in range(3)]
    return jnp.concatenate(rows, axis=0), chosen


def dot_transposed(left, right):
    return lax.dot_general(left, right, (((1,), (1,)), ((), ())), preferred_element_type=F32)


OWN_UNROLL = 32


def own_kernel(gaussians, index_hbm, send_ref, basis_ref, params, rows_ref, table_ref, index_ref, sems, index_sem):
    def fetch(k):
        return pltpu.make_async_copy(
            gaussians.at[:, pl.ds(pl.multiple_of(k * LANES, LANES), LANES)],
            params.at[pl.ds(pl.multiple_of(k * PAD_PARAMS, PAD_PARAMS), PARAMS), :],
            sems.at[k],
        )

    def start(k, carry):
        fetch(k).start()
        return carry

    lax.fori_loop(0, OWNED // LANES, start, 0)
    index_copy = pltpu.make_async_copy(index_hbm, index_ref, index_sem)
    index_copy.start()

    def group(kb, carry):
        for k in range(8):
            fetch(8 * kb + k).wait()

        def param(a):
            return params[pl.ds(kb * 8 * PAD_PARAMS + a, 8, stride=PAD_PARAMS), :]

        attributes, basis = project(param)
        for a in range(ATTRS):
            rows_ref[pl.ds(kb * 8 * ATTRS + a, 8, stride=ATTRS), :] = attributes[a]
        for k in range(16):
            basis_ref[pl.ds(kb * 8 * 16 + k, 8, stride=16), :] = basis[k]
        return carry

    lax.fori_loop(0, OWNED // LANES // 8, group, 0)
    build_table(rows_ref, table_ref, Q_OWN)
    index_copy.wait()

    def blocks(i, carry):
        index_rows = index_ref[pl.ds(pl.multiple_of(2 * OWN_UNROLL * i, 8), 2 * OWN_UNROLL), :]
        base = pl.multiple_of(i * (18 * OWN_UNROLL), 8)
        for group in range(OWN_UNROLL // 4):
            found = gather_lanes(index_rows[8 * group : 8 * group + 8], rows_ref, FORM, OWNED // LANES)
            for a, values in zip(FORM, found):
                send_ref[pl.ds(base + 8 * ATTRS * group + a, 8, stride=ATTRS), :] = values
        for j in range(OWN_UNROLL):
            entries = jnp.concatenate([index_rows[2 * j : 2 * j + 1], index_rows[2 * j + 1 : 2 * j + 2]], axis=1)
            picked = gather_block(entries, table_ref, Q_OWN)
            for half in range(2):
                row = base + 18 * j + 9 * half
                lanes = slice(LANES * half, LANES * half + LANES)
                send_ref[pl.ds(row, 5), :] = picked[:5, lanes]
                send_ref[pl.ds(row + 8, 1), :] = picked[5:6, lanes]
        return carry

    lax.fori_loop(0, PEERS // 2 // OWN_UNROLL, blocks, 0)


GATHER_UNROLL = 16
RENDER_UNROLL = 8
MOST = TILE_DEV * BLOCKS
LISTED = MOST + 16


def render_kernel(
    received,
    slots_ref,
    cot_ref,
    counts_ref,
    rank_ref,
    image_ref,
    grad_ref,
    table_ref,
    triangle_ref,
    entries_ref,
    attr_ref,
    halves_ref,
    form_ref,
    gone_ref,
    total_ref,
    picture_ref,
    listed,
):
    build_table(received, table_ref, Q_SLOT)
    before = lax.broadcasted_iota(jnp.int32, (UNIT, UNIT), 0)
    after = lax.broadcasted_iota(jnp.int32, (UNIT, UNIT), 1)
    triangle = jnp.where(before < after, 1.0, 0.0).astype(BF16)
    triangle_ref[...] = triangle
    picture_ref[...] = jnp.zeros_like(picture_ref)
    total_ref[...] = jnp.zeros_like(total_ref)

    live = jnp.int32(0)
    for t in range(TILE_DEV):
        for b in range(BLOCKS):
            listed[live + b] = t * 8 + b
            row = slots_ref[t, pl.ds(b, 1), :]
            entries_ref[live + b] = row
            for half in range(2):
                halves_ref[pl.ds(2 * (live + b) + half, 1), :] = row[:, LANES * half : LANES * half + LANES]
        live = live + counts_ref[t]
    for extra in range(16):
        listed[live + extra] = TILE_DEV * 8
        entries_ref[live + extra] = jnp.zeros((1, UNIT), jnp.int32)
        halves_ref[pl.ds(2 * (live + extra), 2), :] = jnp.zeros((2, LANES), jnp.int32)

    def gather_step(i, carry):
        for group in range(GATHER_UNROLL // 4):
            row = pl.multiple_of(i * (2 * GATHER_UNROLL), 8) + 8 * group
            found = gather_lanes(halves_ref[pl.ds(row, 8), :], received, FORM, PEERS)
            for index in range(3):
                form_ref[index, pl.ds(row, 8), :] = found[index]
        for j in range(GATHER_UNROLL):
            n = i * GATHER_UNROLL + j
            attr_ref[n] = gather_block(entries_ref[n], table_ref, Q_SLOT)
        return carry

    lax.fori_loop(0, (live + GATHER_UNROLL - 1) // GATHER_UNROLL, gather_step, 0)

    rank = rank_ref[0]
    lane_ones = jnp.zeros((5, UNIT), F32)
    across = lax.broadcasted_iota(jnp.int32, (8, UNIT), 0).astype(F32)

    def render_one(n):
        code = listed[n]
        t = code >> 3
        source = jnp.minimum(t, TILE_DEV - 1)
        first = (code & 7) == 0
        local_tile = (rank * TILE_DEV + t) % 256
        origin_x = (16 * (local_tile % 16)).astype(F32) + 0.5
        origin_y = (16 * (local_tile // 16)).astype(F32) + 0.5
        picked = attr_ref[n]

        def wide(row):
            return jnp.broadcast_to(picked[row : row + 1], (8, UNIT))

        centre_u, centre_v = wide(2), wide(3)
        def form(index):
            halves = [form_ref[index, pl.ds(2 * n + half, 1), :] for half in range(2)]
            return jnp.broadcast_to(jnp.concatenate(halves, axis=1), (8, UNIT))

        form_a = form(0) * (-0.5 * LOG2E)
        form_b = form(1) * (-LOG2E)
        form_c = form(2) * (-0.5 * LOG2E)
        log_opacity = wide(4)
        constant, linear = [], []
        for half in range(2):
            delta_x = (across + (origin_x + 8.0 * half)) - centre_u
            constant.append(form_a * delta_x * delta_x + log_opacity)
            linear.append(form_b * delta_x)
        powers = []
        for y in range(16):
            delta_y = (origin_y + y) - centre_v
            bent = form_c * delta_y
            for half in range(2):
                powers.append(constant[half] + delta_y * (linear[half] + bent))
        alpha = jnp.exp2(jnp.concatenate(powers, axis=0))
        log_keep = jnp.log2(1.0 - alpha)
        sums = jnp.dot(jnp.concatenate(split_two(log_keep), axis=0), triangle_ref[...], preferred_element_type=F32)
        cot = jnp.concatenate([cot_ref[c, pl.ds(source, 1), :] for c in range(3)] + [lane_ones], axis=0)
        cot_columns = [jnp.transpose(jnp.broadcast_to(cot[c : c + 1], (LANES, UNIT))) for c in range(3)]
        kept = jnp.where(first, 0.0, 1.0)
        back = [[jnp.zeros((8, LANES), F32) for half in range(2)] for c in range(3)]
        weights = []
        for p in range(UNIT // 8):
            rows = slice(8 * p, 8 * p + 8)
            gone = gone_ref[pl.ds(8 * p, 8), :] * kept
            earlier = (sums[rows] + sums[UNIT + 8 * p : UNIT + 8 * p + 8]) + jnp.concatenate([gone, gone], axis=1)
            weight = alpha[rows] * jnp.exp2(earlier)
            last = (earlier + log_keep[rows])[:, UNIT - 1 : UNIT]
            gone_ref[pl.ds(8 * p, 8), :] = jnp.broadcast_to(last, (8, LANES))
            weights.append(weight)
        for c in range(3):
            for p in range(UNIT // 8):
                column = cot_columns[c][8 * p : 8 * p + 8]
                for half in range(2):
                    back[c][half] += column * weights[p][:, LANES * half : LANES * half + LANES]
        weight_high, weight_low = split_two(jnp.concatenate(weights, axis=0))
        columns = jnp.concatenate([picked[0:2], picked[5:6], lane_ones], axis=0)
        colour_high, colour_low = split_two(columns)
        nothing = jnp.zeros((8, UNIT), BF16)
        left = jnp.concatenate(
            [
                jnp.concatenate([colour_high, colour_low], axis=0),
                jnp.concatenate([colour_high, nothing], axis=0),
            ],
            axis=1,
        )
        seen = dot_transposed(left, jnp.concatenate([weight_high, weight_low], axis=1))
        seen = seen[:8] + seen[8:]
        picture_ref[t] = jnp.where(first, seen, picture_ref[t] + seen)
        sums_back = [
            jnp.sum(jnp.concatenate(back[c], axis=1), axis=0, keepdims=True) for c in range(3)
        ]
        return jnp.where(t < TILE_DEV, jnp.concatenate(sums_back, axis=0), 0.0)

    def scatter_pair(n, values):
        lefts, rights = [], []
        for j in range(RENDER_UNROLL):
            left, right = scatter_terms(entries_ref[n + j], values[j], Q_SLOT)
            lefts.append(left)
            rights.append(right)
        total_ref[...] += dot_transposed(jnp.concatenate(lefts, axis=1), jnp.concatenate(rights, axis=1))

    def render_step(i, values):
        n = i * RENDER_UNROLL
        scatter_pair(jnp.maximum(n - RENDER_UNROLL, 0), values)
        return tuple(render_one(n + j) for j in range(RENDER_UNROLL))

    gone_ref[...] = jnp.zeros_like(gone_ref)
    steps = (live + RENDER_UNROLL - 1) // RENDER_UNROLL
    nothing_back = tuple(jnp.zeros((3, UNIT), F32) for j in range(RENDER_UNROLL))
    values = lax.fori_loop(0, steps, render_step, nothing_back)
    scatter_pair((steps - 1) * RENDER_UNROLL, values)
    for c in range(3):
        for half in range(2):
            lanes = pl.ds(half * LANES, LANES)
            grad_ref[pl.ds(3 * half + c, Q_SLOT, stride=6), :] = (
                total_ref[pl.ds(c * Q_SLOT, Q_SLOT), lanes]
                + total_ref[pl.ds((3 + c) * Q_SLOT, Q_SLOT), lanes]
            )
    for t in range(TILE_DEV):
        for c in range(3):
            image_ref[c, pl.ds(t, 1), :] = picture_ref[t, pl.ds(c, 1), :]


FINISH_UNROLL = 32


def finish_kernel(returned, index_ref, basis_ref, out_ref, total_ref):
    total_ref[...] = jnp.zeros_like(total_ref)

    def scatter_step(i, carry):
        rows = returned[pl.ds(pl.multiple_of(i * (6 * FINISH_UNROLL), 8), 6 * FINISH_UNROLL), :]
        index_rows = index_ref[pl.ds(pl.multiple_of(2 * FINISH_UNROLL * i, 8), 2 * FINISH_UNROLL), :]
        lefts, rights = [], []
        for j in range(FINISH_UNROLL):
            entries = jnp.concatenate([index_rows[2 * j : 2 * j + 1], index_rows[2 * j + 1 : 2 * j + 2]], axis=1)
            values = jnp.concatenate([rows[6 * j : 6 * j + 3], rows[6 * j + 3 : 6 * j + 6]], axis=1)
            left, right = scatter_terms(entries, values, Q_OWN)
            lefts.append(left)
            rights.append(right)
        total_ref[...] += dot_transposed(jnp.concatenate(lefts, axis=1), jnp.concatenate(rights, axis=1))
        return carry

    lax.fori_loop(0, PEERS // 2 // FINISH_UNROLL, scatter_step, 0)
    for k in range(OWNED // LANES):
        basis = basis_ref[pl.ds(16 * k, 16), :]
        for c in range(3):
            lanes = pl.ds((k % 2) * LANES, LANES)
            grad = (
                total_ref[pl.ds(c * Q_OWN + k // 2, 1), lanes]
                + total_ref[pl.ds((3 + c) * Q_OWN + k // 2, 1), lanes]
            )
            out_ref[pl.ds(16 * c, 16), pl.ds(k * LANES, LANES)] = basis * grad


def exchange(buffer):
    return lax.all_to_all(buffer, AXES, split_axis=0, concat_axis=0, tiled=True)


def per_device(gaussians, send_index, tile_slots, block_count, cotangent):
    vmem = pl.BlockSpec(memory_space=pltpu.VMEM)
    smem = pl.BlockSpec(memory_space=pltpu.SMEM)
    limits = pltpu.CompilerParams(vmem_limit_bytes=VMEM_BYTES)
    shape = jax.ShapeDtypeStruct
    rank = lax.axis_index(AXES).astype(jnp.int32).reshape(1)
    index = send_index.reshape(PEERS, WIDTH)
    send, basis = pl.pallas_call(
        own_kernel,
        out_shape=(shape((ATTRS * PEERS, WIDTH), F32), shape((16 * OWNED // LANES, LANES), F32)),
        in_specs=[pl.BlockSpec(memory_space=pltpu.HBM), pl.BlockSpec(memory_space=pltpu.HBM)],
        out_specs=(vmem, vmem),
        scratch_shapes=[
            pltpu.VMEM((PAD_PARAMS * OWNED // LANES, LANES), F32),
            pltpu.VMEM((ATTRS * OWNED // LANES, LANES), F32),
            pltpu.VMEM((16 * Q_OWN, UNIT), BF16),
            pltpu.VMEM((PEERS, WIDTH), jnp.int32),
            pltpu.SemaphoreType.DMA((OWNED // LANES,)),
            pltpu.SemaphoreType.DMA(()),
        ],
        compiler_params=pltpu.CompilerParams(vmem_limit_bytes=62 * 2**20),
        name="project_and_pack",
    )(gaussians, index)
    received = exchange(send.reshape(PEERS, ATTRS * WIDTH)).reshape(ATTRS * PEERS, WIDTH)
    image, slot_grad = pl.pallas_call(
        render_kernel,
        out_shape=(shape((3, TILE_DEV, UNIT), F32), shape((3 * PEERS, WIDTH), F32)),
        in_specs=[vmem, vmem, vmem, smem, smem],
        out_specs=(vmem, vmem),
        scratch_shapes=[
            pltpu.VMEM((16 * Q_SLOT, UNIT), BF16),
            pltpu.VMEM((UNIT, UNIT), BF16),
            pltpu.VMEM((LISTED, 1, UNIT), jnp.int32),
            pltpu.VMEM((LISTED, 8, UNIT), F32),
            pltpu.VMEM((2 * LISTED, LANES), jnp.int32),
            pltpu.VMEM((3, 2 * LISTED, LANES), F32),
            pltpu.VMEM((UNIT, LANES), F32),
            pltpu.VMEM((6 * Q_SLOT, UNIT), F32),
            pltpu.VMEM((TILE_DEV + 1, 8, UNIT), F32),
            pltpu.SMEM((LISTED,), jnp.int32),
        ],
        compiler_params=limits,
        name="render",
    )(received, tile_slots, cotangent, block_count, rank)
    returned = exchange(slot_grad.reshape(PEERS, 3 * WIDTH)).reshape(3 * PEERS, WIDTH)
    sh_grad = pl.pallas_call(
        finish_kernel,
        out_shape=shape((48, OWNED), F32),
        in_specs=[vmem, vmem, vmem],
        out_specs=vmem,
        scratch_shapes=[pltpu.VMEM((6 * Q_OWN, UNIT), F32)],
        compiler_params=limits,
        name="finish",
    )(returned, index, basis)
    return image, sh_grad


def solution(mesh):
    placed = (
        P(None, AXES),
        P(AXES, None, None),
        P(AXES, None, None),
        P(AXES),
        P(None, AXES, None),
    )
    return jax.shard_map(
        per_device,
        mesh=mesh,
        in_specs=placed,
        out_specs=(P(None, AXES, None), P(None, AXES)),
        check_vma=False,
    )
```
